256 devices in a mesh: grp: 2 (over z_hi), tile: 32 (over x, y, core), lev: 4 (over z_lo).
Axes of the slice: x: 4, y: 4, z: 8 (z_hi: 2, z_lo: 4; z = z_hi * 4 + z_lo), core: 2. Of those that a mesh axis runs over, the one named last changes fastest.
Arguments:
- members: bfloat16 [16, 8, 1536, 3072], P('grp', 'lev', 'tile'), may hold values from -6 to 6
- obs_value: float32 [8, 1536, 3072], P('lev', 'tile'), may hold values from -6 to 6
- obs_count: int32 [1536, 3072], P('tile'), may hold values from 0 to 4
- variance: float32 [8, 768], P('lev'), may hold values from 0.1 to 4
- wave_order: int32 [768], replicated, may hold values from 0 to 767, each once
Outputs:
- recentered: bfloat16 [16, 8, 1536, 3072], P('grp', 'lev', 'tile')
- control: float32 [4, 2, 2, 768, 768], P('lev', 'grp', None, 'tile')
The draws below stay inside these ranges and needn't reach their ends.
Inputs may be any that keep to these rules, and one draw needn't show every extreme that they name: `wave_order`: each wavenumber 0 to 767 stands in exactly one slot.
All inputs are finite; a program needn't handle non-finite values.
Results may differ from the reference program's by a relative error of at most 0.001.
Values sent between devices are 32-bit elements; how exact they have to be, the bound alone decides.
No kernel may reach another device: no remote copies, remote signals or barrier semaphores. Data moves between devices by JAX's collectives and lax.ppermute only.
A program may use at most 128 MiB of HBM per device.

```python
import math
import jax
import jax.numpy as jnp
from jax import lax

NLAT = 1536
NLON = 3072
MW = 768
NDEG = 768
MEM = 16
ITERS = 2
LEVS = 8


def touch_ends(array, stream_key, smallest, high):
    longest = array.shape.index(max(array.shape))
    spots = []
    for shift in (0, 1):
        where = [jax.random.randint(jax.random.fold_in(stream_key, axis), (), 0, length) for axis, length in enumerate(array.shape)]
        where[longest] = (where[longest] + shift) % array.shape[longest]
        spots.append(tuple(where))
    return array.at[spots[0]].set(smallest).at[spots[1]].set(high)


def block_levels(own_key, extent, cuts, least, high):
    gain = 1.0
    for position, shards_of in cuts:
        draws = jax.random.uniform(jax.random.fold_in(jax.random.fold_in(own_key, 6), position), (shards_of,), jnp.float32, least / len(cuts), high / len(cuts))
        gain = gain * jnp.repeat(jnp.exp(draws), extent[position] // shards_of).reshape((-1,) + (1,) * (len(extent) - 1 - position))
    return gain


def centred(stream_key, dims, spread, bound, pieces=(), held_as=jnp.bfloat16):
    entries = jax.random.normal(stream_key, dims, jnp.float32) * spread
    if len(pieces) > 0:
        entries = block_levels(stream_key, dims, pieces, -0.22, 0.18) * entries
    return jnp.clip(entries, min=-bound, max=bound).astype(held_as)


def setup_inputs(seed: int = 0) -> dict:
    key_list = jax.random.split(jax.random.key(seed), 6)
    members = centred(key_list[0], (MEM, LEVS, NLAT, NLON), 1.0, 6.0, ((0, 2), (1, 4), (2, 32)))
    obs_value = centred(key_list[1], (LEVS, NLAT, NLON), 1.0, 6.0, ((0, 4), (1, 32)), jnp.float32)
    obs_count = touch_ends(jax.random.randint(key_list[2], (NLAT, NLON), 0, 5), jax.random.fold_in(key_list[2], 1), 0, 4).astype(jnp.int32)
    variance = jnp.clip(jnp.exp(math.log(4.0) - 3.6888794 * jax.random.uniform(key_list[3], (LEVS, NDEG), jnp.float32) ** block_levels(key_list[3], (LEVS, NDEG), ((0, 4),), -0.2, 0.2)), 0.1, 4.0)
    wave_order = jax.random.permutation(key_list[4], MW).astype(jnp.int32)
    return {"members": members, "obs_value": obs_value, "obs_count": obs_count, "variance": variance, "wave_order": wave_order}


SPREAD_FACTOR = 1.2
HIGH = lax.Precision.HIGHEST

def zonal_basis(wave_order, lon_count):
    positions = jnp.arange(lon_count, dtype=jnp.int32)
    turn_index = wave_order.astype(jnp.int32)[:, None] * positions[None, :] % lon_count
    angles = turn_index.astype(jnp.float32) * (2.0 * math.pi / lon_count)
    factor = math.sqrt(2.0 / lon_count)
    return jnp.stack([jnp.cos(angles), jnp.sin(angles)]) * factor

def latitude_basis(degrees, lat_rows):
    degree_index = jnp.arange(degrees, dtype=jnp.int32)
    odd_rows = 2 * jnp.arange(lat_rows, dtype=jnp.int32) + 1
    turn_index = degree_index[:, None] * odd_rows[None, :] % (4 * lat_rows)
    angles = turn_index.astype(jnp.float32) * (math.pi / (2.0 * lat_rows))
    return jnp.cos(angles) * math.sqrt(2.0 / lat_rows)

def reference(members, obs_value, obs_count, variance, wave_order):
    zonal_rows = zonal_basis(wave_order, NLON)
    latitude = latitude_basis(NDEG, NLAT)
    live_mask = jnp.arange(NDEG, dtype=jnp.int32)[None, :] >= wave_order.astype(jnp.int32)[:, None]
    spec_scale = jnp.where(live_mask[None, :, :], jnp.sqrt(variance)[:, None, :], jnp.float32(0.0))
    ensemble_mean = lax.optimization_barrier(jnp.sum(members, axis=0, dtype=jnp.float32)) / MEM
    weights = obs_count.astype(jnp.float32) * 0.5

    def to_spectral(grid_field):
        coeffs = jnp.einsum('csi,lji->lcsj', zonal_rows, grid_field, precision=HIGH)
        return jnp.einsum('lcsj,nj->lcsn', coeffs, latitude, precision=HIGH) * spec_scale[:, None]

    def to_grid(spectral):
        lat_values = jnp.einsum('lcsn,nj->lcsj', spectral * spec_scale[:, None], latitude, precision=HIGH)
        return jnp.einsum('lcsj,csi->lji', lat_values, zonal_rows, precision=HIGH)
    rhs = to_spectral(weights[None] * (obs_value - ensemble_mean))
    control = jnp.zeros_like(rhs)
    analysis_increment = jnp.zeros_like(ensemble_mean)
    residual = rhs
    direction = rhs
    norm_now = jnp.sum(residual * residual)
    for solver_iteration in range(ITERS):
        field_now = to_grid(direction)
        image_vec = direction + to_spectral(weights[None] * field_now)
        step_len = norm_now / jnp.sum(direction * image_vec)
        control = control + step_len * direction
        analysis_increment = analysis_increment + step_len * field_now
        residual = residual - step_len * image_vec
        norm_next = jnp.sum(residual * residual)
        direction = residual + norm_next / norm_now * direction
        norm_now = norm_next
    member_offset = ensemble_mean + analysis_increment - SPREAD_FACTOR * ensemble_mean
    recentered = (SPREAD_FACTOR * members.astype(jnp.float32) + member_offset[None]).astype(jnp.bfloat16)
    control_out = control.reshape(LEVS // 2, 2, 2, MW, NDEG)
    return (recentered, control_out)
```

```python
import functools
import math
import numpy as np
import jax
import jax.numpy as jnp
import ml_dtypes
from jax import lax
from jax.experimental import pallas as pl
from jax.experimental.pallas import tpu as pltpu
from jax.sharding import PartitionSpec as P

BF = jnp.bfloat16
F32 = jnp.float32
MEM = 16
SPREAD_FACTOR = 1.2
PARAMS = pltpu.CompilerParams(vmem_limit_bytes=56 * 2**20)


def split_table(table):
    high = table.astype(ml_dtypes.bfloat16)
    low = (table - high.astype(np.float64)).astype(ml_dtypes.bfloat16)
    return np.stack([high, low])


def zonal_tables(waves, lon_count):
    quarter = lon_count // 4
    columns = quarter + 128
    place = np.arange(columns)
    parts = []
    for parity in (0, 1):
        m = np.arange(parity, waves, 2)
        turn = (m[:, None] * place[None, :]) % lon_count
        angle = turn * (2.0 * math.pi / lon_count)
        for wave in (np.cos(angle), np.sin(angle)):
            wave = wave * math.sqrt(2.0 / lon_count)
            wave[:, quarter + 1 :] = 0.0
            parts.append(split_table(wave))
    return np.stack(parts)


def latitude_table(degrees, bands, rows):
    lat_count = bands * rows
    n = np.arange(degrees)
    out = np.zeros((degrees, bands, 64))
    j = np.arange(lat_count)
    turn = (n[:, None] * (2 * j + 1)[None, :]) % (4 * lat_count)
    out[:, :, :rows] = (np.cos(turn * (math.pi / (2.0 * lat_count))) * math.sqrt(2.0 / lat_count)).reshape(degrees, bands, rows)
    return split_table(out.reshape(degrees, bands * 64))


def halves(x):
    high = x.astype(BF)
    return high, (x - high.astype(F32)).astype(BF)


def lanes_like(x):
    return lax.broadcasted_iota(jnp.int32, x.shape, x.ndim - 1)


def flip_shift(x):
    lanes = lanes_like(x)
    return jnp.take_along_axis(x, (128 - lanes) % 128, axis=-1)


def block(x, q):
    return x[:, 128 * q : 128 * (q + 1)]


def mirrored(x, top, count, keep_first):
    out = []
    for q in range(count):
        body = flip_shift(block(x, top - 1 - q))
        first = lanes_like(body) == 0
        if q == 0 and not keep_first:
            out.append(jnp.where(first, 0.0, body))
        else:
            out.append(jnp.where(first, block(x, top - q), body))
    return jnp.concatenate(out, axis=1)


NT = (((1,), (1,)), ((), ()))
NN = (((1,), (0,)), ((), ()))
TN = (((0,), (0,)), ((), ()))


def dot(a, b, dims=NN):
    return lax.dot_general(a, b, dims, preferred_element_type=F32)


def fold(grid):
    q = grid.shape[1] // 4
    blocks = q // 128
    rows = grid.shape[0]
    zero = jnp.zeros((rows, 128), F32)
    a = grid[:, : q + 128]
    c = grid[:, 2 * q : 3 * q + 128]
    b = jnp.concatenate([mirrored(grid, 2 * blocks, blocks, False), zero], axis=1)
    d = jnp.concatenate([mirrored(grid, 4 * blocks, blocks, False), zero], axis=1)
    ac, bd, amc, bmd = a + c, b + d, a - c, b - d
    return ac + bd, ac - bd, amc - bmd, amc + bmd


def analyse(grid, table_ref, perm):
    rows = grid.shape[0]
    pad = jnp.zeros((64 - rows, grid.shape[1] // 4 + 128), BF)
    parts = fold(grid)
    natural = []
    for parity in (0, 1):
        sums = []
        for c in (0, 1):
            high, low = halves(parts[2 * parity + c])
            both = jnp.concatenate([high, pad, low, pad], axis=0)
            if c == 1:
                both = jnp.concatenate([low, pad, high, pad], axis=0)
            acc = dot(table_ref[2 * parity + c, 0], both, NT) + dot(table_ref[2 * parity + c, 1], both, NT)
            sums.append(acc + pltpu.roll(acc, 64, 1))
        natural.append(jnp.where(lanes_like(sums[0]) < 64, sums[0], sums[1]))
    natural = jnp.concatenate(natural, axis=0)
    high, low = halves(natural)
    moved = dot(perm, jnp.concatenate([high, low], axis=1))
    return moved[:, :128] + moved[:, 128:]


def place_of(wave, waves):
    return wave // 2 + (wave % 2) * (waves // 2)


def one_hot(place, axis, waves):
    return (lax.broadcasted_iota(jnp.int32, (waves, waves), axis) == place).astype(F32).astype(BF)


def synthesise(band, table_ref, perm_t, rows, lon):
    q = lon // 4
    blocks = q // 128
    waves = band.shape[0]
    high, low = halves(band)
    moved = dot(perm_t, jnp.concatenate([high, low], axis=1))
    natural = moved[:, :128] + moved[:, 128:]
    parts = []
    for parity in (0, 1):
        flipped = natural[parity * (waves // 2) : (parity + 1) * (waves // 2)].T
        high, low = halves(flipped)
        for c in (0, 1):
            lhs = jnp.concatenate([high[64 * c : 64 * c + 64], low[64 * c : 64 * c + 64]], axis=0)
            acc = dot(lhs, table_ref[2 * parity + c, 0]) + dot(lhs, table_ref[2 * parity + c, 1])
            parts.append(acc[:rows] + acc[64 : 64 + rows])
    ce, se, co, so = parts
    f1 = (ce + co + se + so)[:, :q]
    a = ce - co - se + so
    f3 = (ce - co + se - so)[:, :q]
    b = ce + co - se - so
    f2 = mirrored(a, blocks, blocks, True)
    f4 = mirrored(b, blocks, blocks, True)
    return jnp.concatenate([f1, f2, f3, f4], axis=1)


def turn(x, by):
    return pltpu.roll(x, by % 128, 1)


def pack(x):
    lanes = lanes_like(x)
    y = jnp.where(lanes < 48, x, turn(x, -16))
    k = x.shape[0] // 4
    a, b, c, d = (y[i * k : (i + 1) * k] for i in range(4))
    lanes = lanes[:k]
    return jnp.concatenate(
        [
            jnp.where(lanes < 96, a, turn(b, 96)),
            jnp.where(lanes < 64, turn(b, -32), turn(c, 64)),
            jnp.where(lanes < 32, turn(c, -64), turn(d, 32)),
        ],
        axis=0,
    )


def unpack(p):
    k = p.shape[0] // 3
    p0, p1, p2 = (p[i * k : (i + 1) * k] for i in range(3))
    lanes = lanes_like(p0)
    y = jnp.concatenate(
        [
            p0,
            jnp.where(lanes < 32, turn(p0, 32), turn(p1, 32)),
            jnp.where(lanes < 64, turn(p1, 64), turn(p2, 64)),
            turn(p2, -32),
        ],
        axis=0,
    )
    lanes = lanes_like(y)
    x = jnp.where(lanes < 48, y, turn(y, 16))
    return jnp.where((lanes < 48) | ((lanes >= 64) & (lanes < 112)), x, 0.0)


def total(x):
    return jnp.sum(jnp.sum(x, axis=0, keepdims=True), axis=1, keepdims=True)


def mark(x, values):
    rows = lax.broadcasted_iota(jnp.int32, x.shape, x.ndim - 2)
    lanes = lanes_like(x)
    for i, value in enumerate(values):
        value = value.reshape((1,) * x.ndim)
        x = jnp.where((rows == 0) & (lanes == 48 + i), value, x)
    return x


def spread(values):
    lanes = lax.broadcasted_iota(jnp.int32, (8, 128), 1)
    out = jnp.zeros((8, 128), F32)
    for i, value in enumerate(values):
        out = jnp.where(lanes == i, value, out)
    return out


def level_sum(members_ref):
    acc = members_ref[0, 0].astype(F32)
    for k in range(1, members_ref.shape[0]):
        acc = acc + members_ref[k, 0].astype(F32)
    return acc


def other_kernel(grp_ref, members_ref, count_ref, order_ref, table_ref, sum_ref, out_ref):
    waves = order_ref.shape[0]
    acc = level_sum(members_ref)
    sum_ref[...] = acc
    weights = count_ref[...].astype(F32) * 0.5
    perm = one_hot(place_of(order_ref[...], waves), 1, waves)
    out_ref[...] = pack(analyse(-weights * (acc / MEM), table_ref, perm))


def own_kernel(grp_ref, members_ref, obs_ref, count_ref, order_ref, table_ref, sum_ref, out_ref):
    waves = order_ref.shape[0]
    acc = level_sum(members_ref)
    sum_ref[...] = acc
    weights = count_ref[...].astype(F32) * 0.5
    perm = one_hot(place_of(order_ref[...], waves), 1, waves)
    out_ref[...] = analyse(weights * (obs_ref[0] - acc / MEM), table_ref, perm)


def join_kernel(own_ref, packed_ref, out_ref):
    out_ref[...] = (own_ref[...] + unpack(packed_ref[...])).reshape(out_ref.shape)


def latitude_analysis(chunks_ref, lat_ref):
    bands, slots, _ = chunks_ref.shape
    cos, sin = [], []
    for p in range(bands // 2):
        x0, x1 = chunks_ref[2 * p], chunks_ref[2 * p + 1]
        lower = lanes_like(x0) < 64
        cos.append(jnp.where(lower, x0, turn(x1, 64)))
        sin.append(jnp.where(lower, turn(x0, 64), x1))
    x = jnp.concatenate([jnp.concatenate(cos, axis=1), jnp.concatenate(sin, axis=1)], axis=0)
    high, low = halves(x)
    lhs = jnp.concatenate([high, low], axis=0)
    acc = dot(lhs, lat_ref[0], NT) + dot(lhs, lat_ref[1], NT)
    return acc[: 2 * slots] + acc[2 * slots :]


def latitude_synthesis(vector, lat_ref, out_ref, values):
    bands, slots, _ = out_ref.shape
    high, low = halves(vector)
    lhs = jnp.concatenate([high, low], axis=0)
    acc = dot(lhs, lat_ref[0]) + dot(lhs, lat_ref[1])
    y = acc[: 2 * slots] + acc[2 * slots :]
    for p in range(bands // 2):
        y0, y1 = block(y[:slots], p), block(y[slots:], p)
        lower = lanes_like(y0) < 64
        out_ref[2 * p] = mark(jnp.where(lower, y0, turn(y1, 64)), values)
        out_ref[2 * p + 1] = mark(jnp.where(lower, turn(y0, 64), y1), values)


def scale_of(variance, waves_col, degrees):
    slots = waves_col.shape[0]
    degree = lax.broadcasted_iota(jnp.int32, (slots, degrees), 1)
    scale = jnp.where(degree >= waves_col, jnp.sqrt(variance), 0.0)
    return jnp.concatenate([scale, scale], axis=0)


def latitude_first_kernel(chunks_ref, variance_ref, waves_ref, lat_ref, rhs_ref, out_ref):
    scale = scale_of(variance_ref[...], waves_ref[...], variance_ref.shape[1])
    rhs = latitude_analysis(chunks_ref, lat_ref) * scale
    rhs_ref[...] = rhs
    latitude_synthesis(rhs * scale, lat_ref, out_ref, [total(rhs * rhs)])


def latitude_second_kernel(chunks_ref, variance_ref, waves_ref, rhs_ref, lat_ref, image_ref, out_ref):
    scale = scale_of(variance_ref[...], waves_ref[...], variance_ref.shape[1])
    image = rhs_ref[...] + latitude_analysis(chunks_ref, lat_ref) * scale
    image_ref[...] = image
    latitude_synthesis(image * scale, lat_ref, out_ref, [])


def grid_kernel(band_ref, count_ref, row_ref, order_ref, table_ref, field_ref, packed_ref, out_ref):
    bands, slots, _ = band_ref.shape
    waves = bands * slots
    rows, lon = count_ref.shape
    band = band_ref[...].reshape(waves, 128)
    packed_ref[...] = pack(band)
    perm_t = one_hot(place_of(row_ref[...], waves), 0, waves)
    field = synthesise(band, table_ref, perm_t, rows, lon)
    field_ref[...] = field
    weighted = count_ref[...].astype(F32) * 0.5 * field
    perm = one_hot(place_of(order_ref[...], waves), 1, waves)
    out = analyse(weighted, table_ref, perm)
    norm = jnp.zeros((1, 1), F32)
    for t in range(bands):
        norm = norm + band_ref[t, 0:1, 48:49]
    out_ref[...] = mark(out.reshape(bands, slots, 128), [total(weighted * field), norm])


def pack_kernel(band_ref, packed_ref):
    bands, slots, _ = band_ref.shape
    packed_ref[...] = pack(band_ref[...].reshape(bands * slots, 128))


def first_step(reduced):
    norm, curve = reduced[0:1, 0:1], reduced[0:1, 1:2]
    return norm / (norm + curve)


def last_kernel(band_ref, count_ref, row_ref, table_ref, field_ref, rhs_ref, image_ref, reduced_ref, next_ref, sums_ref):
    bands, slots, _ = band_ref.shape
    waves = bands * slots
    rows, lon = count_ref.shape
    perm_t = one_hot(place_of(row_ref[...], waves), 0, waves)
    field = synthesise(band_ref[...].reshape(waves, 128), table_ref, perm_t, rows, lon)
    step = first_step(reduced_ref[...])
    start = field_ref[...]
    following = start - step * field
    next_ref[...] = following
    weighted = count_ref[...].astype(F32) * 0.5 * following
    rhs = rhs_ref[...]
    residual = rhs - step * image_ref[...]
    sums_ref[...] = spread([total(residual * residual), total(residual * rhs), total(weighted * following), total(weighted * start)])


def partner_first_kernel(packed_ref, row_ref, table_ref, field_ref):
    waves = row_ref.shape[1]
    rows, lon = field_ref.shape
    perm_t = one_hot(place_of(row_ref[...], waves), 0, waves)
    field_ref[...] = synthesise(unpack(packed_ref[...]), table_ref, perm_t, rows, lon)


def partner_second_kernel(packed_ref, row_ref, table_ref, start_ref, reduced_ref, next_ref):
    waves = row_ref.shape[1]
    rows, lon = next_ref.shape
    perm_t = one_hot(place_of(row_ref[...], waves), 0, waves)
    field = synthesise(unpack(packed_ref[...]), table_ref, perm_t, rows, lon)
    next_ref[...] = start_ref[...] - first_step(reduced_ref[...]) * field


def finish_kernel(grp_ref, members_ref, sa_ref, sb_ref, start_ref, next_ref, reduced_ref, sums_ref, rhs_ref, image_ref, out_ref, control_ref):
    reduced, sums = reduced_ref[...], sums_ref[...]
    norm, field_norm = reduced[0:1, 0:1], reduced[0:1, 1:2]
    step = first_step(reduced)
    norm_next, cross, field_next, field_cross = (sums[0:1, i : i + 1] for i in range(4))
    ratio = norm_next / norm
    curve = norm_next + field_next + 2.0 * ratio * (cross + field_cross) + ratio * ratio * (norm + field_norm)
    step_next = norm_next / curve
    mean = (sa_ref[0] + sb_ref[0]) / MEM
    start = start_ref[0]
    increment = step * start + step_next * (next_ref[0] + ratio * start)
    offset = (mean + increment) - SPREAD_FACTOR * mean
    for k in range(members_ref.shape[0]):
        out_ref[k, 0] = (SPREAD_FACTOR * members_ref[k, 0].astype(F32) + offset).astype(BF)
    rhs = rhs_ref[...]
    residual = rhs - step * image_ref[...]
    control_ref[...] = step * rhs + step_next * (residual + ratio * rhs)


def shape(*dims):
    return jax.ShapeDtypeStruct(dims, F32)


def call(kernel, outs, name):
    return pl.pallas_call(kernel, out_shape=outs, compiler_params=PARAMS, name=name)


def butterfly(value, axis, count):
    step = 1
    while step < count:
        value = value + lax.ppermute(value, axis, [(i, i ^ step) for i in range(count)])
        step *= 2
    return value


def on_device(tables, lat_table, members, obs_value, obs_count, variance, wave_order):
    grp = lax.axis_index("grp")
    bands = lax.axis_size("tile")
    levels = lax.axis_size("lev")
    mem, _, rows, lon = members.shape
    waves = wave_order.shape[0]
    slots = waves // bands
    degrees = variance.shape[1]
    swap = [(0, 1), (1, 0)]
    own_waves = lax.dynamic_slice_in_dim(wave_order, lax.axis_index("tile") * slots, slots, 0)[:, None]
    own_variance = lax.dynamic_index_in_dim(variance, grp, 0, keepdims=True)
    order_col, order_row = wave_order[:, None], wave_order[None, :]
    grp_scalar = grp[None].astype(jnp.int32)

    def whole(array):
        return pl.BlockSpec(array.shape, lambda i, g: (0,) * array.ndim)

    def start_call(kernel, arrays, specs, outs, flip, name):
        member_spec = pl.BlockSpec((mem, 1, rows, lon), lambda i, g: (0, g[0] ^ flip, 0, 0))
        return pl.pallas_call(
            kernel,
            grid_spec=pltpu.PrefetchScalarGridSpec(
                num_scalar_prefetch=1,
                grid=(1,),
                in_specs=[member_spec] + specs,
                out_specs=[whole(o) for o in outs],
            ),
            out_shape=outs,
            compiler_params=PARAMS,
            name=name,
        )(grp_scalar, members, *arrays)

    chunk = shape(bands, slots, 128)
    packed = shape(waves * 3 // 4, 128)
    field = shape(rows, lon)
    vector = shape(2 * slots, degrees)
    with jax.named_scope("start"):
        sum_other, coeffs_other = start_call(
            other_kernel, (obs_count, order_col, tables), [whole(obs_count), whole(order_col), whole(tables)], [field, packed], 1, "other"
        )
        coeffs_in = lax.ppermute(coeffs_other, "grp", swap)
        obs_spec = pl.BlockSpec((1, rows, lon), lambda i, g: (g[0], 0, 0))
        sum_own, coeffs_own = start_call(
            own_kernel,
            (obs_value, obs_count, order_col, tables),
            [obs_spec, whole(obs_count), whole(order_col), whole(tables)],
            [field, shape(waves, 128)],
            0,
            "own",
        )
        sum_own_in = lax.ppermute(sum_other, "grp", swap)
        sum_other_in = lax.ppermute(sum_own, "grp", swap)
        coeffs = call(join_kernel, chunk, "join")(coeffs_own, coeffs_in)

    def exchange(chunks):
        return lax.all_to_all(chunks, "tile", 0, 0, tiled=True)

    with jax.named_scope("solve"):
        rhs, lat_values = call(latitude_first_kernel, [vector, chunk], "lat1")(exchange(coeffs), own_variance, own_waves, lat_table)
        field_own, packed_first, coeffs = call(grid_kernel, [field, packed, chunk], "grid")(
            exchange(lat_values), obs_count, order_row, order_col, tables
        )
        packed_first_in = lax.ppermute(packed_first, "grp", swap)
        arrived = exchange(coeffs)
        norm = arrived[0, 0:1, 49:50]
        curve = jnp.sum(arrived[:, 0, 48]).reshape(1, 1)
        reduced = butterfly(jnp.pad(jnp.concatenate([norm, curve], axis=1), ((0, 7), (0, 126))), "lev", levels)
        reduced = butterfly(reduced, "grp", 2)
        image, lat_values = call(latitude_second_kernel, [vector, chunk], "lat2")(arrived, own_variance, own_waves, rhs, lat_table)
        band = exchange(lat_values)
        packed_second_in = lax.ppermute(call(pack_kernel, packed, "pack")(band), "grp", swap)
        next_own, sums = call(last_kernel, [field, shape(8, 128)], "last")(
            band, obs_count, order_row, tables, field_own, rhs, image, reduced
        )
        sums = butterfly(sums, "tile", bands)
        sums = butterfly(sums, "lev", levels)
        sums = butterfly(sums, "grp", 2)
        field_other = call(partner_first_kernel, field, "partner1")(packed_first_in, order_row, tables)
        next_other = call(partner_second_kernel, field, "partner2")(packed_second_in, order_row, tables, field_other, reduced)

    with jax.named_scope("finish"):
        cut = 16

        def own_first(*dims):
            return pl.BlockSpec(dims, lambda h, r, g: (h ^ g[0], r, 0))

        def fixed(*dims):
            return pl.BlockSpec(dims, lambda h, r, g: (0,) * len(dims))

        member_spec = pl.BlockSpec((mem, 1, cut, lon), lambda h, r, g: (0, h, r, 0))
        piece = own_first(1, cut, lon)
        small = fixed(8, 128)
        vec = fixed(2 * slots, degrees)
        recentered, control = pl.pallas_call(
            finish_kernel,
            grid_spec=pltpu.PrefetchScalarGridSpec(
                num_scalar_prefetch=1,
                grid=(2, rows // cut),
                in_specs=[member_spec, piece, piece, piece, piece, small, small, vec, vec],
                out_specs=[member_spec, vec],
            ),
            out_shape=[jax.ShapeDtypeStruct(members.shape, BF), vector],
            compiler_params=PARAMS,
            name="finish",
        )(
            grp_scalar,
            members,
            jnp.stack([sum_own, sum_other]),
            jnp.stack([sum_own_in, sum_other_in]),
            jnp.stack([field_own, field_other]),
            jnp.stack([next_own, next_other]),
            reduced,
            sums,
            rhs,
            image,
        )
    return recentered, control.reshape(1, 1, 2, slots, degrees)


def solution(mesh):
    bands = mesh.shape["tile"]
    waves, degrees, rows, lon = 768, 768, 48, 3072
    tables = zonal_tables(waves, lon)
    lat_table = latitude_table(degrees, bands, rows)
    placed = (
        P("grp", "lev", "tile", None),
        P("lev", "tile", None),
        P("tile", None),
        P("lev", None),
        P(),
    )
    return jax.shard_map(
        lambda *args: on_device(jnp.asarray(tables), jnp.asarray(lat_table), *args),
        mesh=mesh,
        in_specs=placed,
        out_specs=(P("grp", "lev", "tile", None), P("lev", "grp", None, "tile", None)),
        check_vma=False,
    )
```

```python
import functools
import math
import numpy as np
import jax
import jax.numpy as jnp
import ml_dtypes
from jax import lax
from jax.experimental import pallas as pl
from jax.experimental.pallas import tpu as pltpu
from jax.sharding import PartitionSpec as P

BF = jnp.bfloat16
F32 = jnp.float32
MEM = 16
SPREAD_FACTOR = 1.2
LARGE_LIMIT = 52


def split_table(table):
    high = table.astype(ml_dtypes.bfloat16)
    low = (table - high.astype(np.float64)).astype(ml_dtypes.bfloat16)
    return np.stack([high, low])


def zonal_tables(waves, lon_count):
    quarter = lon_count // 4
    columns = quarter + 128
    place = np.arange(columns)
    parts = []
    for parity in (0, 1):
        m = np.arange(parity, waves, 2)
        turn = (m[:, None] * place[None, :]) % lon_count
        angle = turn * (2.0 * math.pi / lon_count)
        for wave in (np.cos(angle), np.sin(angle)):
            wave = wave * math.sqrt(2.0 / lon_count)
            wave[:, quarter + 1 :] = 0.0
            parts.append(split_table(wave))
    return np.stack(parts)


def latitude_table(degrees, bands, rows):
    lat_count = bands * rows
    n = np.arange(degrees)
    out = np.zeros((degrees, bands, 64))
    j = np.arange(lat_count)
    turn = (n[:, None] * (2 * j + 1)[None, :]) % (4 * lat_count)
    out[:, :, :rows] = (np.cos(turn * (math.pi / (2.0 * lat_count))) * math.sqrt(2.0 / lat_count)).reshape(degrees, bands, rows)
    return split_table(out.reshape(degrees, bands * 64))


class Loaded:
    def __init__(self, source, scratch, semaphores, indices, ahead=4):
        self.scratch = scratch
        self.copies = {
            index: pltpu.make_async_copy(source.at[index], scratch.at[index], semaphores.at[place])
            for place, index in enumerate(indices)
        }
        self.to_start = list(indices)
        self.to_wait = set(indices)
        for _ in range(ahead):
            self.start_next()

    def start_next(self):
        if self.to_start:
            self.copies[self.to_start.pop(0)].start()

    def __getitem__(self, index):
        if index in self.to_wait:
            while index in self.to_start:
                self.start_next()
            self.copies[index].wait()
            self.to_wait.remove(index)
            self.start_next()
        return self.scratch[index]


GROUPS = [(group, part) for group in range(4) for part in range(2)]


def halves(x):
    high = x.astype(BF)
    return high, (x - high.astype(F32)).astype(BF)


def lanes_like(x):
    return lax.broadcasted_iota(jnp.int32, x.shape, x.ndim - 1)


def flip_shift(x):
    lanes = lanes_like(x)
    return jnp.take_along_axis(x, (128 - lanes) % 128, axis=-1)


def block(x, q):
    return x[:, 128 * q : 128 * (q + 1)]


def mirrored(x, top, count, keep_first):
    out = []
    for q in range(count):
        body = flip_shift(block(x, top - 1 - q))
        first = lanes_like(body) == 0
        if q == 0 and not keep_first:
            out.append(jnp.where(first, 0.0, body))
        else:
            out.append(jnp.where(first, block(x, top - q), body))
    return jnp.concatenate(out, axis=1)


NT = (((1,), (1,)), ((), ()))
NN = (((1,), (0,)), ((), ()))
TN = (((0,), (0,)), ((), ()))


def dot(a, b, dims=NN):
    return lax.dot_general(a, b, dims, preferred_element_type=F32)


def fold(grid):
    q = grid.shape[1] // 4
    blocks = q // 128
    rows = grid.shape[0]
    zero = jnp.zeros((rows, 128), F32)
    a = grid[:, : q + 128]
    c = grid[:, 2 * q : 3 * q + 128]
    b = jnp.concatenate([mirrored(grid, 2 * blocks, blocks, False), zero], axis=1)
    d = jnp.concatenate([mirrored(grid, 4 * blocks, blocks, False), zero], axis=1)
    ac, bd, amc, bmd = a + c, b + d, a - c, b - d
    return ac + bd, ac - bd, amc - bmd, amc + bmd


def analyse(grid, table, perm):
    rows = grid.shape[0]
    pad = jnp.zeros((64 - rows, grid.shape[1] // 4 + 128), BF)
    parts = fold(grid)
    natural = []
    for parity in (0, 1):
        sums = []
        for c in (0, 1):
            high, low = halves(parts[2 * parity + c])
            both = jnp.concatenate([high, pad, low, pad], axis=0)
            if c == 1:
                both = jnp.concatenate([low, pad, high, pad], axis=0)
            acc = dot(table[2 * parity + c, 0], both, NT) + dot(table[2 * parity + c, 1], both, NT)
            sums.append(acc + pltpu.roll(acc, 64, 1))
        natural.append(jnp.where(lanes_like(sums[0]) < 64, sums[0], sums[1]))
    natural = jnp.concatenate(natural, axis=0)
    high, low = halves(natural)
    moved = dot(perm, jnp.concatenate([high, low], axis=1))
    return moved[:, :128] + moved[:, 128:]


def place_of(wave, waves):
    return wave // 2 + (wave % 2) * (waves // 2)


def to_natural(order_row):
    waves = order_row.shape[1]
    hit = lax.broadcasted_iota(jnp.int32, (waves, waves), 0) == place_of(order_row, waves)
    return hit.astype(F32).astype(BF)


def to_slots(order_row):
    waves = order_row.shape[1]
    place = jnp.broadcast_to(place_of(order_row, waves).astype(F32), (128, waves)).T
    lanes = lanes_like(place)
    hits = [(place == (lanes + first).astype(F32)).astype(F32).astype(BF) for first in range(0, waves, 128)]
    return jnp.concatenate(hits, axis=1)


def synthesise(band, table, perm_t, rows, lon):
    q = lon // 4
    blocks = q // 128
    waves = band.shape[0]
    high, low = halves(band)
    moved = dot(perm_t, jnp.concatenate([high, low], axis=1))
    natural = moved[:, :128] + moved[:, 128:]
    parts = []
    for parity in (0, 1):
        flipped = natural[parity * (waves // 2) : (parity + 1) * (waves // 2)].T
        high, low = halves(flipped)
        for c in (0, 1):
            lhs = jnp.concatenate([high[64 * c : 64 * c + 64], low[64 * c : 64 * c + 64]], axis=0)
            acc = dot(lhs, table[2 * parity + c, 0]) + dot(lhs, table[2 * parity + c, 1])
            parts.append(acc[:rows] + acc[64 : 64 + rows])
    ce, se, co, so = parts
    f1 = (ce + co + se + so)[:, :q]
    a = ce - co - se + so
    f3 = (ce - co + se - so)[:, :q]
    b = ce + co - se - so
    f2 = mirrored(a, blocks, blocks, True)
    f4 = mirrored(b, blocks, blocks, True)
    return jnp.concatenate([f1, f2, f3, f4], axis=1)


def turn(x, by):
    return pltpu.roll(x, by % 128, 1)


def pack(x):
    lanes = lanes_like(x)
    y = jnp.where(lanes < 48, x, turn(x, -16))
    k = x.shape[0] // 4
    a, b, c, d = (y[i * k : (i + 1) * k] for i in range(4))
    lanes = lanes[:k]
    return jnp.concatenate(
        [
            jnp.where(lanes < 96, a, turn(b, 96)),
            jnp.where(lanes < 64, turn(b, -32), turn(c, 64)),
            jnp.where(lanes < 32, turn(c, -64), turn(d, 32)),
        ],
        axis=0,
    )


def unpack(p):
    k = p.shape[0] // 3
    p0, p1, p2 = (p[i * k : (i + 1) * k] for i in range(3))
    lanes = lanes_like(p0)
    y = jnp.concatenate(
        [
            p0,
            jnp.where(lanes < 32, turn(p0, 32), turn(p1, 32)),
            jnp.where(lanes < 64, turn(p1, 64), turn(p2, 64)),
            turn(p2, -32),
        ],
        axis=0,
    )
    lanes = lanes_like(y)
    x = jnp.where(lanes < 48, y, turn(y, 16))
    return jnp.where((lanes < 48) | ((lanes >= 64) & (lanes < 112)), x, 0.0)


def total(x):
    return jnp.sum(jnp.sum(x, axis=0, keepdims=True), axis=1, keepdims=True)


def mark(x, values):
    rows = lax.broadcasted_iota(jnp.int32, x.shape, x.ndim - 2)
    lanes = lanes_like(x)
    for i, value in enumerate(values):
        value = value.reshape((1,) * x.ndim)
        x = jnp.where((rows == 0) & (lanes == 48 + i), value, x)
    return x


def spread(values, level):
    lanes = lax.broadcasted_iota(jnp.int32, (1, 128), 1)
    out = jnp.zeros((1, 128), F32)
    for i, value in enumerate(values):
        out = jnp.where(lanes == 8 * i + level, value, out)
    return out


def quantities(row, count):
    lanes = lanes_like(row)
    return [jnp.where(lanes < 8, turn(row, -8 * i), 0.0) for i in range(count)]


def level_sum(members_ref, level, held, semaphores):
    count = members_ref.shape[0]
    copies = [pltpu.make_async_copy(members_ref.at[k, level], held.at[k], semaphores.at[k]) for k in range(count)]
    for copy in copies:
        copy.start()

    def finish():
        acc = None
        for k in range(count):
            copies[k].wait()
            value = held[k].astype(F32)
            acc = value if acc is None else acc + value
        return acc

    return finish


PIECES = 3


def other_kernel(grp_ref, members_ref, count_ref, row_ref, table_ref, out_ref, sum_ref, held, held_table, sums_sem, table_sem):
    summed = level_sum(members_ref, 1 - grp_ref[0], held, sums_sem)
    table = Loaded(table_ref, held_table, table_sem, GROUPS)
    perm = to_slots(row_ref[...])
    acc = summed()
    sum_ref[...] = acc
    weights = count_ref[...].astype(F32) * 0.5
    out_ref[...] = pack(analyse(-weights * (acc / MEM), table, perm))


def own_kernel(grp_ref, members_ref, obs_ref, count_ref, row_ref, table_ref, out_ref, sum_ref, held, held_table, held_obs, sums_sem, table_sem, obs_sem):
    summed = level_sum(members_ref, grp_ref[0], held, sums_sem)
    obs = pltpu.make_async_copy(obs_ref.at[grp_ref[0]], held_obs, obs_sem)
    obs.start()
    table = Loaded(table_ref, held_table, table_sem, GROUPS)
    perm = to_slots(row_ref[...])
    acc = summed()
    sum_ref[...] = acc
    weights = count_ref[...].astype(F32) * 0.5
    obs.wait()
    out_ref[...] = analyse(weights * (held_obs[...] - acc / MEM), table, perm)


def join_kernel(own_ref, packed_ref, sum_own_ref, sum_other_ref, out_ref, sum_own_out, sum_other_out):
    out_ref[...] = (own_ref[...] + unpack(packed_ref[...])).reshape(out_ref.shape)


LAT_PIECES = 3


def load_latitude(lat_ref, held, semaphores):
    return Loaded(lat_ref, held, semaphores, [(piece, part) for piece in range(LAT_PIECES) for part in range(2)])


def latitude_analysis(chunks_ref, lat):
    bands, slots, _ = chunks_ref.shape
    cos, sin = [], []
    for p in range(bands // 2):
        x0, x1 = chunks_ref[2 * p], chunks_ref[2 * p + 1]
        lower = lanes_like(x0) < 64
        cos.append(jnp.where(lower, x0, turn(x1, 64)))
        sin.append(jnp.where(lower, turn(x0, 64), x1))
    x = jnp.concatenate([jnp.concatenate(cos, axis=1), jnp.concatenate(sin, axis=1)], axis=0)
    high, low = halves(x)
    lhs = jnp.concatenate([high, low], axis=0)
    pieces = []
    for piece in range(LAT_PIECES):
        acc = dot(lhs, lat[piece, 0], NT) + dot(lhs, lat[piece, 1], NT)
        pieces.append(acc[: 2 * slots] + acc[2 * slots :])
    return jnp.concatenate(pieces, axis=1)


def latitude_synthesis(vector, lat, out_ref, values):
    bands, slots, _ = out_ref.shape
    high, low = halves(vector)
    lhs = jnp.concatenate([high, low], axis=0)
    cut = vector.shape[1] // LAT_PIECES
    acc = 0.0
    for piece in range(LAT_PIECES):
        part = lhs[:, piece * cut : (piece + 1) * cut]
        acc = acc + dot(part, lat[piece, 0]) + dot(part, lat[piece, 1])
    y = acc[: 2 * slots] + acc[2 * slots :]
    for p in range(bands // 2):
        y0, y1 = block(y[:slots], p), block(y[slots:], p)
        lower = lanes_like(y0) < 64
        out_ref[2 * p] = mark(jnp.where(lower, y0, turn(y1, 64)), values)
        out_ref[2 * p + 1] = mark(jnp.where(lower, turn(y0, 64), y1), values)


def scale_of(variance, waves_col, degrees):
    slots = waves_col.shape[0]
    degree = lax.broadcasted_iota(jnp.int32, (slots, degrees), 1)
    scale = jnp.where(degree >= waves_col, jnp.sqrt(variance), 0.0)
    return jnp.concatenate([scale, scale], axis=0)


def latitude_first_kernel(chunks_ref, variance_ref, waves_ref, lat_ref, *refs):
    rhs_ref, out_ref, held, semaphores = refs[-4:]
    lat = load_latitude(lat_ref, held, semaphores)
    scale = scale_of(variance_ref[...], waves_ref[...], variance_ref.shape[1])
    rhs = latitude_analysis(chunks_ref, lat) * scale
    rhs_ref[...] = rhs
    latitude_synthesis(rhs * scale, lat, out_ref, [total(rhs * rhs)])


def latitude_second_kernel(chunks_ref, variance_ref, waves_ref, rhs_ref, lat_ref, *refs):
    image_ref, out_ref, quotient_ref, held, semaphores = refs[-5:]
    lat = load_latitude(lat_ref, held, semaphores)
    norm, field_norm = chunks_ref[0, 0:1, 49:50], marks(chunks_ref, 48)
    extra = jnp.where(norm > 0.0, field_norm / norm, 0.0)
    quotient_ref[...] = jnp.broadcast_to(1.0 + extra, (8, 128))
    scale = scale_of(variance_ref[...], waves_ref[...], variance_ref.shape[1])
    image = latitude_analysis(chunks_ref, lat) * scale - extra * rhs_ref[...]
    image_ref[...] = image
    latitude_synthesis(image * scale, lat, out_ref, [])


def marks(band_ref, lane):
    value = jnp.zeros((1, 1), F32)
    for t in range(band_ref.shape[0]):
        value = value + band_ref[t, 0:1, lane : lane + 1]
    return value


def grid_kernel(band_ref, count_ref, row_ref, table_ref, *refs):
    field_ref, out_ref, held, semaphores = refs[-4:]
    table = Loaded(table_ref, held, semaphores, GROUPS)
    bands, slots, _ = band_ref.shape
    rows, lon = count_ref.shape
    row = row_ref[...]
    field = synthesise(band_ref[...].reshape(bands * slots, 128), table, to_natural(row), rows, lon)
    field_ref[...] = field
    weighted = count_ref[...].astype(F32) * 0.5 * field
    out = analyse(weighted, table, to_slots(row)).reshape(bands, slots, 128)
    out_ref[...] = mark(out, [total(weighted * field), marks(band_ref, 48)])


def last_kernel(level_ref, band_ref, count_ref, row_ref, table_ref, field_ref, rhs_ref, image_ref, quotient_ref, *refs):
    next_ref, sums_ref, held, semaphores = refs[-4:]
    table = Loaded(table_ref, held, semaphores, GROUPS)
    bands, slots, _ = band_ref.shape
    rows, lon = count_ref.shape
    rhs, image, start = rhs_ref[...], image_ref[...], field_ref[...]
    weights = count_ref[...].astype(F32) * 0.5
    field = synthesise(band_ref[...].reshape(bands * slots, 128), table, to_natural(row_ref[...]), rows, lon)
    next_ref[...] = field
    weighted = weights * field
    row = spread(
        [
            total(rhs * rhs),
            total(weights * start * start),
            total(image * image),
            total(image * rhs),
            total(weighted * field),
            total(weighted * start),
            quotient_ref[0:1, 0:1] / bands,
        ],
        level_ref[0],
    )
    sums_ref[...] = jnp.broadcast_to(row[None], sums_ref.shape)


def combine_kernel(level_ref, sums_ref, sums_in_ref, rhs_ref, image_ref, first_ref, second_ref, control_ref, packed_ref, factors_ref):
    bands, slots, _ = first_ref.shape
    sums = sums_ref[...] + sums_in_ref[...]
    norm, field_norm, image_norm, cross, next_norm, field_cross, quotient = quantities(sums, 7)

    def over_levels(x):
        return jnp.sum(x, axis=1, keepdims=True)

    norm_all, field_all = over_levels(norm), over_levels(field_norm)
    step = norm_all / (norm_all + field_all)
    keep = 1.0 - step * quotient
    norm_next = over_levels(keep * keep * norm - 2.0 * step * keep * cross + step * step * image_norm)
    field_next = over_levels(keep * keep * field_norm - 2.0 * step * keep * field_cross + step * step * next_norm)
    mixed = over_levels(keep * (norm + field_norm) - step * (cross + field_cross))
    ratio = norm_next / norm_all
    curve = norm_next + field_next + 2.0 * ratio * mixed + ratio * ratio * (norm_all + field_all)
    step_next = norm_next / curve
    mine = lanes_like(keep) == level_ref[0]
    first = over_levels(jnp.where(mine, step + step_next * (keep + ratio), 0.0))
    second = -step_next * step
    control_ref[...] = first * rhs_ref[...] + second * image_ref[...]
    band = first * first_ref[...].reshape(bands * slots, 128) + second * second_ref[...].reshape(bands * slots, 128)
    packed_ref[...] = pack(band)
    lanes = lanes_like(sums)
    factors_ref[...] = jnp.where(lanes == 0, first, jnp.where(lanes == 1, second, 0.0))


class Recentering:
    def __init__(self, members_ref, level, sums, out_ref, scratch):
        self.near, self.near_sums, self.held, near_sem, sums_sem, self.out_sem = scratch
        self.out_ref, self.level = out_ref, level
        rows = members_ref.shape[2]
        self.cut = rows // PIECES
        self.loads = []
        for piece in range(PIECES):
            source = members_ref.at[:, level, pl.ds(piece * self.cut, self.cut)]
            self.loads.append(pltpu.make_async_copy(source, self.near.at[piece], near_sem.at[piece]))
        self.sum_loads = [
            pltpu.make_async_copy(source.at[index], self.near_sums.at[k], sums_sem.at[k]) for k, (source, index) in enumerate(sums)
        ]
        for copy in self.sum_loads + self.loads:
            copy.start()

    def run(self, increment):
        for copy in self.sum_loads:
            copy.wait()
        copies = []
        for piece in range(PIECES):
            here = slice(piece * self.cut, (piece + 1) * self.cut)
            mean = (self.near_sums[0, here] + self.near_sums[1, here]) / MEM
            offset = (mean + increment(here)) - SPREAD_FACTOR * mean
            self.loads[piece].wait()
            for k in range(self.near.shape[1]):
                self.held[piece, k] = (SPREAD_FACTOR * self.near[piece, k].astype(F32) + offset).astype(BF)
            target = self.out_ref.at[:, self.level, pl.ds(piece * self.cut, self.cut)]
            copies.append(pltpu.make_async_copy(self.held.at[piece], target, self.out_sem.at[piece]))
            copies[-1].start()
        for copy in copies:
            copy.wait()


def finish_own_kernel(grp_ref, members_ref, sums_own_ref, sums_other_ref, factors_ref, start_ref, next_ref, out_ref, *scratch):
    me = grp_ref[0]
    work = Recentering(members_ref, me, ((sums_own_ref, me), (sums_other_ref, 1 - me)), out_ref, scratch)
    first, second = factors_ref[0:1, 0:1], factors_ref[0:1, 1:2]
    work.run(lambda here: first * start_ref[here] + second * next_ref[here])


def finish_other_kernel(grp_ref, members_ref, sums_own_ref, sums_other_ref, packed_ref, row_ref, table_ref, half_ref, out_ref, *scratch):
    held_table, table_sem, scratch = scratch[0], scratch[1], scratch[2:]
    table = Loaded(table_ref, held_table, table_sem, GROUPS)
    me = grp_ref[0]
    work = Recentering(members_ref, 1 - me, ((sums_own_ref, 1 - me), (sums_other_ref, me)), out_ref, scratch)
    rows, lon = members_ref.shape[2:]
    field = synthesise(unpack(packed_ref[...]), table, to_natural(row_ref[...]), rows, lon)
    work.run(lambda here: field[here])


def shape(*dims):
    return jax.ShapeDtypeStruct(dims, F32)


def call(kernel, outs, name, hbm=(), hbm_outs=(), scalars=(), aliases=None, scratch=(), limit=LARGE_LIMIT):
    def run(*args):
        def space(i, far, scalars=()):
            return pltpu.SMEM if i in scalars else pltpu.HBM if i in far else pltpu.VMEM

        return pl.pallas_call(
            kernel,
            out_shape=outs,
            in_specs=[pl.BlockSpec(memory_space=space(i, hbm, scalars)) for i in range(len(args))],
            out_specs=[pl.BlockSpec(memory_space=space(o, hbm_outs)) for o in range(len(outs))],
            input_output_aliases=aliases or {},
            scratch_shapes=scratch,
            compiler_params=pltpu.CompilerParams(vmem_limit_bytes=limit * 2**20),
            cost_estimate=pl.CostEstimate(flops=1, bytes_accessed=1, transcendentals=0),
            name=name,
        )(*args)

    return run


def butterfly(value, axis, count):
    step = 1
    while step < count:
        value = value + lax.ppermute(value, axis, [(i, i ^ step) for i in range(count)])
        step *= 2
    return value


def on_device(tables, lat_table, members, obs_value, obs_count, variance, wave_order):
    grp = lax.axis_index("grp")
    bands = lax.axis_size("tile")
    levels = lax.axis_size("lev")
    mem, _, rows, lon = members.shape
    waves = wave_order.shape[0]
    slots = waves // bands
    degrees = variance.shape[1]
    swap = [(0, 1), (1, 0)]
    own_waves = lax.dynamic_slice_in_dim(wave_order, lax.axis_index("tile") * slots, slots, 0)[:, None]
    own_variance = lax.dynamic_index_in_dim(variance, grp, 0, keepdims=True)
    row = wave_order[None, :]
    grp_scalar = grp[None].astype(jnp.int32)

    chunk = shape(bands, slots, 128)
    packed = shape(waves * 3 // 4, 128)
    field = shape(rows, lon)
    vector = shape(2 * slots, degrees)
    small = shape(8, 128)
    dma = pltpu.SemaphoreType.DMA
    zonal = [pltpu.VMEM(tables.shape, BF), dma((len(GROUPS),))]
    latitude = [pltpu.VMEM(lat_table.shape, BF), dma((2 * LAT_PIECES,))]
    level = pltpu.VMEM((mem, rows, lon), BF)
    cut = rows // PIECES
    level_scalar = (2 * lax.axis_index("lev") + grp)[None].astype(jnp.int32)

    def trade(array):
        return lax.ppermute(array, "grp", swap)

    with jax.named_scope("start"):
        coeffs_other, sum_other = call(
            other_kernel, [packed, field], "other", (1, 4), scalars=(0,), scratch=[level, zonal[0], dma((mem,)), zonal[1]]
        )(grp_scalar, members, obs_count, row, tables)
        coeffs_in = trade(coeffs_other)
        coeffs_own, sum_own = call(
            own_kernel,
            [shape(waves, 128), field],
            "own",
            (1, 2, 5),
            scalars=(0,),
            scratch=[level, zonal[0], pltpu.VMEM((rows, lon), F32), dma((mem,)), zonal[1], dma],
        )(grp_scalar, members, obs_value, obs_count, row, tables)
        coeffs, sum_own, sum_other = call(join_kernel, [chunk, field, field], "join", (2, 3), (1, 2), aliases={2: 1, 3: 2})(
            coeffs_own, coeffs_in, sum_own, sum_other
        )
        sums_own = lax.all_gather(sum_own, "grp")
        sums_other = lax.all_gather(sum_other, "grp")

    def exchange(chunks):
        return lax.all_to_all(chunks, "tile", 0, 0, tiled=True)

    with jax.named_scope("solve"):
        rhs, lat_values = call(latitude_first_kernel, [vector, chunk], "lat1", (3,), scratch=latitude)(
            exchange(coeffs), own_variance, own_waves, lat_table
        )
        band_first = exchange(lat_values)
        field_own, coeffs = call(grid_kernel, [field, chunk], "grid", (3,), scratch=zonal)(
            band_first, obs_count, row, tables
        )
        image, lat_values, quotient = call(latitude_second_kernel, [vector, chunk, small], "lat2", (4,), scratch=latitude)(
            exchange(coeffs), own_variance, own_waves, rhs, lat_table
        )
        band_second = exchange(lat_values)
        sum_row = jax.ShapeDtypeStruct((bands, 1, 128), F32)
        next_own, sums = call(last_kernel, [field, sum_row], "last", (4,), scalars=(0,), scratch=zonal)(
            level_scalar, band_second, obs_count, row, tables, field_own, rhs, image, quotient
        )
        sums = jnp.sum(exchange(sums), axis=0)
        sums = sums + sum(lax.ppermute(sums, "lev", [(i, (i + k) % levels) for i in range(levels)]) for k in range(1, levels))

    with jax.named_scope("finish"):
        control, control_band, factors = call(combine_kernel, [vector, packed, shape(1, 128)], "combine", scalars=(0,), limit=16)(
            level_scalar, sums, trade(sums), rhs, image, band_first, band_second
        )
        control_band = trade(control_band)
        near = pltpu.VMEM((PIECES, mem, cut, lon), BF)
        scratch = [near, pltpu.VMEM((2, rows, lon), F32), near, dma((PIECES,)), dma((2,)), dma((PIECES,))]
        whole_out = jax.ShapeDtypeStruct(members.shape, BF)
        (half,) = call(finish_own_kernel, [whole_out], "finish_own", (1, 2, 3), (0,), scalars=(0,), scratch=scratch, limit=56)(
            grp_scalar, members, sums_own, sums_other, factors, field_own, next_own
        )
        (recentered,) = call(
            finish_other_kernel, [whole_out], "finish_other", (1, 2, 3, 6, 7), (0,), scalars=(0,), aliases={7: 0}, scratch=zonal + scratch, limit=56
        )(grp_scalar, members, sums_own, sums_other, control_band, row, tables, half)
    return recentered, control.reshape(1, 1, 2, slots, degrees)


def solution(mesh):
    bands = mesh.shape["tile"]
    waves, degrees, rows, lon = 768, 768, 48, 3072
    tables = zonal_tables(waves, lon)
    lat_table = latitude_table(degrees, bands, rows)
    lat_table = lat_table.reshape(2, LAT_PIECES, degrees // LAT_PIECES, -1).swapaxes(0, 1)
    placed = (
        P("grp", "lev", "tile", None),
        P("lev", "tile", None),
        P("tile", None),
        P("lev", None),
        P(),
    )
    return jax.shard_map(
        lambda *args: on_device(jnp.asarray(tables), jnp.asarray(lat_table), *args),
        mesh=mesh,
        in_specs=placed,
        out_specs=(P("grp", "lev", "tile", None), P("lev", "grp", None, "tile", None)),
        check_vma=False,
    )
```

```python
import functools
import math
import numpy as np
import jax
import jax.numpy as jnp
import ml_dtypes
from jax import lax
from jax.experimental import pallas as pl
from jax.experimental.pallas import tpu as pltpu
from jax.sharding import PartitionSpec as P

BF = jnp.bfloat16
F32 = jnp.float32
MEM = 16
ROWS = 48
SPREAD_FACTOR = 1.2
LARGE_LIMIT = 52


def split_table(table):
    high = table.astype(ml_dtypes.bfloat16)
    low = (table - high.astype(np.float64)).astype(ml_dtypes.bfloat16)
    return np.stack([high, low])


def zonal_tables(waves, lon_count):
    quarter = lon_count // 4
    columns = quarter + 128
    place = np.arange(columns)
    parts = []
    for parity in (0, 1):
        m = np.arange(parity, waves, 2)
        turn = (m[:, None] * place[None, :]) % lon_count
        angle = turn * (2.0 * math.pi / lon_count)
        for wave in (np.cos(angle), np.sin(angle)):
            wave = wave * math.sqrt(2.0 / lon_count)
            wave[:, quarter + 1 :] = 0.0
            parts.append(split_table(wave))
    return np.stack(parts)


def latitude_table(degrees, bands, rows):
    lat_count = bands * rows
    turn_index = (np.arange(degrees)[:, None] * (2 * np.arange(lat_count // 2) + 1)[None, :]) % (4 * lat_count)
    values = np.cos(turn_index * (math.pi / (2.0 * lat_count))) * math.sqrt(2.0 / lat_count)
    out = np.zeros((degrees, bands // 2, 64))
    out[:, :, :rows] = values.reshape(degrees, bands // 2, rows)
    out = out.reshape(degrees, -1)
    return np.stack([split_table(out[0::2]), split_table(out[1::2])])


class Loaded:
    def __init__(self, source, scratch, semaphores, indices, ahead=4):
        self.scratch = scratch
        self.copies = {
            index: pltpu.make_async_copy(source.at[index], scratch.at[index], semaphores.at[place])
            for place, index in enumerate(indices)
        }
        self.to_start = list(indices)
        self.to_wait = set(indices)
        for _ in range(ahead):
            self.start_next()

    def start_next(self):
        if self.to_start:
            self.copies[self.to_start.pop(0)].start()

    def __getitem__(self, index):
        if index in self.to_wait:
            while index in self.to_start:
                self.start_next()
            self.copies[index].wait()
            self.to_wait.remove(index)
            self.start_next()
        return self.scratch[index]


GROUPS = [(group, part) for group in range(4) for part in range(2)]


def halves(x):
    high = x.astype(BF)
    return high, (x - high.astype(F32)).astype(BF)


def lanes_like(x):
    return lax.broadcasted_iota(jnp.int32, x.shape, x.ndim - 1)


def flip_shift(x):
    lanes = lanes_like(x)
    return jnp.take_along_axis(x, (128 - lanes) % 128, axis=-1)


def block(x, q):
    return x[:, 128 * q : 128 * (q + 1)]


def mirrored(x, top, count, keep_first):
    out = []
    for q in range(count):
        body = flip_shift(block(x, top - 1 - q))
        first = lanes_like(body) == 0
        if q == 0 and not keep_first:
            out.append(jnp.where(first, 0.0, body))
        else:
            out.append(jnp.where(first, block(x, top - q), body))
    return jnp.concatenate(out, axis=1)


NT = (((1,), (1,)), ((), ()))
NN = (((1,), (0,)), ((), ()))
TN = (((0,), (0,)), ((), ()))


def dot(a, b, dims=NN):
    return lax.dot_general(a, b, dims, preferred_element_type=F32)


def fold(grid):
    q = grid.shape[1] // 4
    blocks = q // 128
    rows = grid.shape[0]
    zero = jnp.zeros((rows, 128), F32)
    a = grid[:, : q + 128]
    c = grid[:, 2 * q : 3 * q + 128]
    b = jnp.concatenate([mirrored(grid, 2 * blocks, blocks, False), zero], axis=1)
    d = jnp.concatenate([mirrored(grid, 4 * blocks, blocks, False), zero], axis=1)
    ac, bd, amc, bmd = a + c, b + d, a - c, b - d
    return ac + bd, ac - bd, amc - bmd, amc + bmd


def analyse(grid, table, perm):
    rows = grid.shape[0]
    pad = jnp.zeros((64 - rows, grid.shape[1] // 4 + 128), BF)
    parts = fold(grid)
    natural = []
    for parity in (0, 1):
        sums = []
        for c in (0, 1):
            high, low = halves(parts[2 * parity + c])
            both = jnp.concatenate([high, pad, low, pad], axis=0)
            if c == 1:
                both = jnp.concatenate([low, pad, high, pad], axis=0)
            acc = dot(table[2 * parity + c, 0], both, NT) + dot(table[2 * parity + c, 1], both, NT)
            sums.append(acc + pltpu.roll(acc, 64, 1))
        natural.append(jnp.where(lanes_like(sums[0]) < 64, sums[0], sums[1]))
    natural = jnp.concatenate(natural, axis=0)
    high, low = halves(natural)
    moved = dot(perm, jnp.concatenate([high, low], axis=1))
    return moved[:, :128] + moved[:, 128:]


def place_of(wave, waves):
    return wave // 2 + (wave % 2) * (waves // 2)


def to_natural(order_row):
    waves = order_row.shape[1]
    hit = lax.broadcasted_iota(jnp.int32, (waves, waves), 0) == place_of(order_row, waves)
    return hit.astype(F32).astype(BF)


def to_slots(order_row):
    waves = order_row.shape[1]
    place = jnp.broadcast_to(place_of(order_row, waves).astype(F32), (128, waves)).T
    lanes = lanes_like(place)
    hits = [(place == (lanes + first).astype(F32)).astype(F32).astype(BF) for first in range(0, waves, 128)]
    return jnp.concatenate(hits, axis=1)


def synthesise(band, table, perm_t, rows, lon):
    q = lon // 4
    blocks = q // 128
    waves = band.shape[0]
    high, low = halves(band)
    moved = dot(perm_t, jnp.concatenate([high, low], axis=1))
    natural = moved[:, :128] + moved[:, 128:]
    parts = []
    for parity in (0, 1):
        flipped = natural[parity * (waves // 2) : (parity + 1) * (waves // 2)].T
        high, low = halves(flipped)
        for c in (0, 1):
            lhs = jnp.concatenate([high[64 * c : 64 * c + 64], low[64 * c : 64 * c + 64]], axis=0)
            acc = dot(lhs, table[2 * parity + c, 0]) + dot(lhs, table[2 * parity + c, 1])
            parts.append(acc[:rows] + acc[64 : 64 + rows])
    ce, se, co, so = parts
    f1 = (ce + co + se + so)[:, :q]
    a = ce - co - se + so
    f3 = (ce - co + se - so)[:, :q]
    b = ce + co - se - so
    f2 = mirrored(a, blocks, blocks, True)
    f4 = mirrored(b, blocks, blocks, True)
    return jnp.concatenate([f1, f2, f3, f4], axis=1)


def turn(x, by):
    return pltpu.roll(x, by % 128, 1)


def pack(x):
    lanes = lanes_like(x)
    y = jnp.where(lanes < 48, x, turn(x, -16))
    k = x.shape[0] // 4
    a, b, c, d = (y[i * k : (i + 1) * k] for i in range(4))
    lanes = lanes[:k]
    return jnp.concatenate(
        [
            jnp.where(lanes < 96, a, turn(b, 96)),
            jnp.where(lanes < 64, turn(b, -32), turn(c, 64)),
            jnp.where(lanes < 32, turn(c, -64), turn(d, 32)),
        ],
        axis=0,
    )


def unpack(p):
    k = p.shape[0] // 3
    p0, p1, p2 = (p[i * k : (i + 1) * k] for i in range(3))
    lanes = lanes_like(p0)
    y = jnp.concatenate(
        [
            p0,
            jnp.where(lanes < 32, turn(p0, 32), turn(p1, 32)),
            jnp.where(lanes < 64, turn(p1, 64), turn(p2, 64)),
            turn(p2, -32),
        ],
        axis=0,
    )
    lanes = lanes_like(y)
    x = jnp.where(lanes < 48, y, turn(y, 16))
    return jnp.where((lanes < 48) | ((lanes >= 64) & (lanes < 112)), x, 0.0)


def total(x):
    return jnp.sum(jnp.sum(x, axis=0, keepdims=True), axis=1, keepdims=True)


def mark(x, values):
    rows = lax.broadcasted_iota(jnp.int32, x.shape, x.ndim - 2)
    lanes = lanes_like(x)
    for i, value in enumerate(values):
        value = value.reshape((1,) * x.ndim)
        x = jnp.where((rows == 0) & (lanes == 48 + i), value, x)
    return x


def spread(values, level):
    lanes = lax.broadcasted_iota(jnp.int32, (1, 128), 1)
    out = jnp.zeros((1, 128), F32)
    for i, value in enumerate(values):
        out = jnp.where(lanes == 8 * i + level, value, out)
    return out


def quantities(row, count):
    lanes = lanes_like(row)
    return [jnp.where(lanes < 8, turn(row, -8 * i), 0.0) for i in range(count)]


def level_sum(members_ref, level, held, semaphores):
    count = members_ref.shape[0]
    copies = [pltpu.make_async_copy(members_ref.at[k, level], held.at[k], semaphores.at[k]) for k in range(count)]
    for copy in copies:
        copy.start()

    def finish():
        acc = None
        for k in range(count):
            copies[k].wait()
            value = held[k].astype(F32)
            acc = value if acc is None else acc + value
        return acc

    return finish


PIECES = 3


HALVES = 1


def store_halves(value, refs):
    cut = refs[0].shape[0]
    for k, ref in enumerate(refs):
        ref[...] = value[k * cut : (k + 1) * cut]


def other_kernel(grp_ref, members_ref, count_ref, row_ref, table_ref, out_ref, sum_ref, held, held_table, sums_sem, table_sem):
    summed = level_sum(members_ref, 1 - grp_ref[0], held, sums_sem)
    table = Loaded(table_ref, held_table, table_sem, GROUPS)
    perm = to_slots(row_ref[...])
    acc = summed()
    store_halves(acc, (sum_ref,))
    weights = count_ref[...].astype(F32) * 0.5
    out_ref[...] = pack(analyse(-weights * (acc / MEM), table, perm))


def own_kernel(grp_ref, members_ref, obs_ref, count_ref, row_ref, table_ref, out_ref, sum_ref, held, held_table, held_obs, sums_sem, table_sem, obs_sem):
    summed = level_sum(members_ref, grp_ref[0], held, sums_sem)
    obs = pltpu.make_async_copy(obs_ref.at[grp_ref[0]], held_obs, obs_sem)
    obs.start()
    table = Loaded(table_ref, held_table, table_sem, GROUPS)
    perm = to_slots(row_ref[...])
    acc = summed()
    store_halves(acc, (sum_ref,))
    weights = count_ref[...].astype(F32) * 0.5
    obs.wait()
    out_ref[...] = analyse(weights * (held_obs[...] - acc / MEM), table, perm)


def join_kernel(own_ref, packed_ref, out_ref):
    out_ref[...] = (own_ref[...] + unpack(packed_ref[...])).reshape(out_ref.shape)


LAT_GROUPS = [(parity, part) for parity in range(2) for part in range(2)]


def southern(x, rows):
    lanes = lanes_like(x)
    index = jnp.where(lanes < rows, rows - 1 - lanes, jnp.where((lanes >= 64) & (lanes < 64 + rows), 127 + rows - lanes, lanes))
    return jnp.take_along_axis(x, index, axis=-1)


def side_by_side(chunks):
    lower = lanes_like(chunks[0]) < 64
    pairs = [(chunks[k], chunks[k + 1]) for k in range(0, len(chunks), 2)]
    cos = [jnp.where(lower, x0, turn(x1, 64)) for x0, x1 in pairs]
    sin = [jnp.where(lower, turn(x0, 64), x1) for x0, x1 in pairs]
    return jnp.concatenate([jnp.concatenate(cos, axis=1), jnp.concatenate(sin, axis=1)], axis=0)


def apart(y):
    slots = y.shape[0] // 2
    out = []
    for p in range(y.shape[1] // 128):
        y0, y1 = block(y[:slots], p), block(y[slots:], p)
        lower = lanes_like(y0) < 64
        out += [jnp.where(lower, y0, turn(y1, 64)), jnp.where(lower, turn(y0, 64), y1)]
    return out


def latitude_analysis(chunks_ref, lat, rows):
    bands, slots, _ = chunks_ref.shape
    north = [chunks_ref[t] for t in range(bands // 2)]
    south = [southern(chunks_ref[bands - 1 - t], rows) for t in range(bands // 2)]
    out = []
    for parity in range(2):
        x = side_by_side([a + b if parity == 0 else a - b for a, b in zip(north, south)])
        lhs = jnp.concatenate(halves(x), axis=0)
        acc = dot(lhs, lat[parity, 0], NT) + dot(lhs, lat[parity, 1], NT)
        out.append(acc[: 2 * slots] + acc[2 * slots :])
    return jnp.concatenate(out, axis=1)


def latitude_synthesis(vector, lat, out_ref, values, rows):
    bands, slots, _ = out_ref.shape
    half = vector.shape[1] // 2
    y = []
    for parity in range(2):
        lhs = jnp.concatenate(halves(vector[:, parity * half : (parity + 1) * half]), axis=0)
        acc = dot(lhs, lat[parity, 0]) + dot(lhs, lat[parity, 1])
        y.append(acc[: 2 * slots] + acc[2 * slots :])
    for t, chunk in enumerate(apart(y[0] + y[1])):
        out_ref[t] = mark(chunk, values)
    for t, chunk in enumerate(apart(y[0] - y[1])):
        out_ref[bands - 1 - t] = mark(southern(chunk, rows), values)


def scale_of(variance, waves_col, degrees):
    slots = waves_col.shape[0]
    lane = lax.broadcasted_iota(jnp.int32, (slots, degrees), 1)
    degree = 2 * (lane % (degrees // 2)) + lane // (degrees // 2)
    scale = jnp.where(degree >= waves_col, jnp.sqrt(variance), 0.0)
    return jnp.concatenate([scale, scale], axis=0)


def latitude_first_kernel(chunks_ref, variance_ref, waves_ref, lat_ref, *refs):
    rhs_ref, out_ref, held, semaphores = refs[-4:]
    lat = Loaded(lat_ref, held, semaphores, LAT_GROUPS)
    scale = scale_of(variance_ref[...], waves_ref[...], variance_ref.shape[1])
    rhs = latitude_analysis(chunks_ref, lat, ROWS) * scale
    rhs_ref[...] = rhs
    latitude_synthesis(rhs * scale, lat, out_ref, [total(rhs * rhs)], ROWS)


def latitude_second_kernel(chunks_ref, variance_ref, waves_ref, rhs_ref, lat_ref, *refs):
    image_ref, out_ref, quotient_ref, held, semaphores = refs[-5:]
    lat = Loaded(lat_ref, held, semaphores, LAT_GROUPS)
    norm, field_norm = chunks_ref[0, 0:1, 49:50], marks(chunks_ref, 48)
    extra = jnp.where(norm > 0.0, field_norm / norm, 0.0)
    quotient_ref[...] = jnp.broadcast_to(1.0 + extra, (8, 128))
    scale = scale_of(variance_ref[...], waves_ref[...], variance_ref.shape[1])
    image = latitude_analysis(chunks_ref, lat, ROWS) * scale - extra * rhs_ref[...]
    image_ref[...] = image
    latitude_synthesis(image * scale, lat, out_ref, [], ROWS)


def marks(band_ref, lane):
    value = jnp.zeros((1, 1), F32)
    for t in range(band_ref.shape[0]):
        value = value + band_ref[t, 0:1, lane : lane + 1]
    return value


def grid_kernel(band_ref, count_ref, row_ref, table_ref, *refs):
    field_ref, out_ref, held, semaphores = refs[-4:]
    table = Loaded(table_ref, held, semaphores, GROUPS)
    bands, slots, _ = band_ref.shape
    rows, lon = count_ref.shape
    row = row_ref[...]
    field = synthesise(band_ref[...].reshape(bands * slots, 128), table, to_natural(row), rows, lon)
    field_ref[...] = field
    weighted = count_ref[...].astype(F32) * 0.5 * field
    out = analyse(weighted, table, to_slots(row)).reshape(bands, slots, 128)
    out_ref[...] = mark(out, [total(weighted * field), marks(band_ref, 48)])


def last_kernel(level_ref, band_ref, count_ref, row_ref, table_ref, field_ref, rhs_ref, image_ref, quotient_ref, *refs):
    next_ref, sums_ref, held, semaphores = refs[-4:]
    table = Loaded(table_ref, held, semaphores, GROUPS)
    bands, slots, _ = band_ref.shape
    rows, lon = count_ref.shape
    rhs, image, start = rhs_ref[...], image_ref[...], field_ref[...]
    weights = count_ref[...].astype(F32) * 0.5
    field = synthesise(band_ref[...].reshape(bands * slots, 128), table, to_natural(row_ref[...]), rows, lon)
    next_ref[...] = field
    weighted = weights * field
    row = spread(
        [
            total(rhs * rhs),
            total(weights * start * start),
            total(image * image),
            total(image * rhs),
            total(weighted * field),
            total(weighted * start),
            quotient_ref[0:1, 0:1] / bands,
        ],
        level_ref[0],
    )
    sums_ref[...] = jnp.broadcast_to(row[None], sums_ref.shape)


def combine_kernel(level_ref, sums_ref, sums_in_ref, rhs_ref, image_ref, first_ref, second_ref, control_ref, packed_ref, factors_ref):
    bands, slots, _ = first_ref.shape
    sums = sums_ref[...] + sums_in_ref[...]
    norm, field_norm, image_norm, cross, next_norm, field_cross, quotient = quantities(sums, 7)

    def over_levels(x):
        return jnp.sum(x, axis=1, keepdims=True)

    norm_all, field_all = over_levels(norm), over_levels(field_norm)
    step = norm_all / (norm_all + field_all)
    keep = 1.0 - step * quotient
    norm_next = over_levels(keep * keep * norm - 2.0 * step * keep * cross + step * step * image_norm)
    field_next = over_levels(keep * keep * field_norm - 2.0 * step * keep * field_cross + step * step * next_norm)
    mixed = over_levels(keep * (norm + field_norm) - step * (cross + field_cross))
    ratio = norm_next / norm_all
    curve = norm_next + field_next + 2.0 * ratio * mixed + ratio * ratio * (norm_all + field_all)
    step_next = norm_next / curve
    mine = lanes_like(keep) == level_ref[0]
    first = over_levels(jnp.where(mine, step + step_next * (keep + ratio), 0.0))
    second = -step_next * step
    control_ref[...] = first * rhs_ref[...] + second * image_ref[...]
    band = first * first_ref[...].reshape(bands * slots, 128) + second * second_ref[...].reshape(bands * slots, 128)
    packed_ref[...] = pack(band)
    lanes = lanes_like(sums)
    factors_ref[...] = jnp.where(lanes == 0, first, jnp.where(lanes == 1, second, 0.0))


class Recentering:
    def __init__(self, members_ref, level, sums, out_ref, scratch):
        self.near, self.near_sums, self.held, near_sem, sums_sem, self.out_sem = scratch
        self.out_ref, self.level = out_ref, level
        rows = members_ref.shape[2]
        self.cut = rows // PIECES
        self.loads = []
        for piece in range(PIECES):
            source = members_ref.at[:, level, pl.ds(piece * self.cut, self.cut)]
            self.loads.append(pltpu.make_async_copy(source, self.near.at[piece], near_sem.at[piece]))
        self.sum_loads = []
        for k, source in enumerate(sums):
            half = source.shape[0]
            target = self.near_sums.at[k // HALVES, pl.ds(k % HALVES * half, half)]
            self.sum_loads.append(pltpu.make_async_copy(source, target, sums_sem.at[k]))
        for copy in self.sum_loads + self.loads:
            copy.start()

    def run(self, increment):
        for copy in self.sum_loads:
            copy.wait()
        copies = []
        for piece in range(PIECES):
            here = slice(piece * self.cut, (piece + 1) * self.cut)
            mean = (self.near_sums[0, here] + self.near_sums[1, here]) / MEM
            offset = (mean + increment(here)) - SPREAD_FACTOR * mean
            self.loads[piece].wait()
            for k in range(self.near.shape[1]):
                self.held[piece, k] = (SPREAD_FACTOR * self.near[piece, k].astype(F32) + offset).astype(BF)
            target = self.out_ref.at[:, self.level, pl.ds(piece * self.cut, self.cut)]
            copies.append(pltpu.make_async_copy(self.held.at[piece], target, self.out_sem.at[piece]))
            copies[-1].start()
        for copy in copies:
            copy.wait()


def finish_own_kernel(grp_ref, members_ref, *refs):
    sums, (factors_ref, start_ref, next_ref, out_ref), scratch = refs[: 2 * HALVES], refs[2 * HALVES : 2 * HALVES + 4], refs[2 * HALVES + 4 :]
    work = Recentering(members_ref, grp_ref[0], sums, out_ref, scratch)
    first, second = factors_ref[0:1, 0:1], factors_ref[0:1, 1:2]
    work.run(lambda here: first * start_ref[here] + second * next_ref[here])


def finish_other_kernel(grp_ref, members_ref, *refs):
    sums, (packed_ref, row_ref, table_ref, half_ref, out_ref) = refs[: 2 * HALVES], refs[2 * HALVES : 2 * HALVES + 5]
    held_table, table_sem, *scratch = refs[2 * HALVES + 5 :]
    table = Loaded(table_ref, held_table, table_sem, GROUPS)
    work = Recentering(members_ref, 1 - grp_ref[0], sums, out_ref, scratch)
    rows, lon = members_ref.shape[2:]
    field = synthesise(unpack(packed_ref[...]), table, to_natural(row_ref[...]), rows, lon)
    work.run(lambda here: field[here])


def shape(*dims):
    return jax.ShapeDtypeStruct(dims, F32)


def call(kernel, outs, name, hbm=(), hbm_outs=(), scalars=(), aliases=None, scratch=(), limit=LARGE_LIMIT):
    def run(*args):
        def space(i, far, scalars=()):
            return pltpu.SMEM if i in scalars else pltpu.HBM if i in far else pltpu.VMEM

        return pl.pallas_call(
            kernel,
            out_shape=outs,
            in_specs=[pl.BlockSpec(memory_space=space(i, hbm, scalars)) for i in range(len(args))],
            out_specs=[pl.BlockSpec(memory_space=space(o, hbm_outs)) for o in range(len(outs))],
            input_output_aliases=aliases or {},
            scratch_shapes=scratch,
            compiler_params=pltpu.CompilerParams(vmem_limit_bytes=limit * 2**20),
            cost_estimate=pl.CostEstimate(flops=1, bytes_accessed=1, transcendentals=0),
            name=name,
        )(*args)

    return run


def on_device(tables, lat_table, members, obs_value, obs_count, variance, wave_order):
    grp = lax.axis_index("grp")
    bands = lax.axis_size("tile")
    levels = lax.axis_size("lev")
    mem, _, rows, lon = members.shape
    waves = wave_order.shape[0]
    slots = waves // bands
    degrees = variance.shape[1]
    swap = [(0, 1), (1, 0)]
    own_waves = lax.dynamic_slice_in_dim(wave_order, lax.axis_index("tile") * slots, slots, 0)[:, None]
    own_variance = lax.dynamic_index_in_dim(variance, grp, 0, keepdims=False)
    own_variance = own_variance.reshape(degrees // 2, 2).T.reshape(1, degrees)
    row = wave_order[None, :]
    grp_scalar = grp[None].astype(jnp.int32)

    chunk = shape(bands, slots, 128)
    packed = shape(waves * 3 // 4, 128)
    field = shape(rows, lon)
    vector = shape(2 * slots, degrees)
    small = shape(8, 128)
    dma = pltpu.SemaphoreType.DMA
    zonal = [pltpu.VMEM(tables.shape, BF), dma((len(GROUPS),))]
    latitude = [pltpu.VMEM(lat_table.shape, BF), dma((len(LAT_GROUPS),))]
    level = pltpu.VMEM((mem, rows, lon), BF)
    cut = rows // PIECES
    halves_out = [shape(rows // HALVES, lon)] * HALVES
    level_scalar = (2 * lax.axis_index("lev") + grp)[None].astype(jnp.int32)

    def trade(array):
        return lax.ppermute(array, "grp", swap)

    with jax.named_scope("start"):
        coeffs_other, *sum_other = call(
            other_kernel, [packed] + halves_out, "other", (1, 4), scalars=(0,), scratch=[level, zonal[0], dma((mem,)), zonal[1]]
        )(grp_scalar, members, obs_count, row, tables)
        coeffs_in = trade(coeffs_other)
        coeffs_own, *sum_own = call(
            own_kernel,
            [shape(waves, 128)] + halves_out,
            "own",
            (1, 2, 5),
            scalars=(0,),
            scratch=[level, zonal[0], pltpu.VMEM((rows, lon), F32), dma((mem,)), zonal[1], dma],
        )(grp_scalar, members, obs_value, obs_count, row, tables)
        (coeffs,) = call(join_kernel, [chunk], "join")(coeffs_own, coeffs_in)
        sum_own_in = [trade(piece) for piece in sum_other]
        sum_other_in = [trade(piece) for piece in sum_own]

    def exchange(chunks):
        return lax.all_to_all(chunks, "tile", 0, 0, tiled=True)

    with jax.named_scope("solve"):
        rhs, lat_values = call(latitude_first_kernel, [vector, chunk], "lat1", (3,), scratch=latitude)(
            exchange(coeffs), own_variance, own_waves, lat_table
        )
        band_first = exchange(lat_values)
        field_own, coeffs = call(grid_kernel, [field, chunk], "grid", (3, 4), scratch=zonal)(
            band_first, obs_count, row, tables, sum_own_in[0]
        )
        image, lat_values, quotient = call(latitude_second_kernel, [vector, chunk, small], "lat2", (4,), scratch=latitude)(
            exchange(coeffs), own_variance, own_waves, rhs, lat_table
        )
        band_second = exchange(lat_values)
        sum_row = jax.ShapeDtypeStruct((bands, 1, 128), F32)
        next_own, sums = call(last_kernel, [field, sum_row], "last", (4,), scalars=(0,), scratch=zonal)(
            level_scalar, band_second, obs_count, row, tables, field_own, rhs, image, quotient
        )
        sums = jnp.sum(exchange(sums), axis=0)
        for step in (1, 2):
            sums = sums + lax.ppermute(sums, "lev", [(i, i ^ step) for i in range(levels)])

    with jax.named_scope("finish"):
        control, control_band, factors = call(combine_kernel, [vector, packed, shape(1, 128)], "combine", scalars=(0,), limit=16)(
            level_scalar, sums, trade(sums), rhs, image, band_first, band_second
        )
        control_band = trade(control_band)
        near = pltpu.VMEM((PIECES, mem, cut, lon), BF)
        scratch = [near, pltpu.VMEM((2, rows, lon), F32), near, dma((PIECES,)), dma((2 * HALVES,)), dma((PIECES,))]
        whole_out = jax.ShapeDtypeStruct(members.shape, BF)
        far = tuple(range(1, 2 + 2 * HALVES))
        (half,) = call(finish_own_kernel, [whole_out], "finish_own", far, (0,), scalars=(0,), scratch=scratch, limit=56)(
            grp_scalar, members, *sum_own, *sum_own_in, factors, field_own, next_own
        )
        last_arg = 5 + 2 * HALVES
        (recentered,) = call(
            finish_other_kernel,
            [whole_out],
            "finish_other",
            far + (last_arg - 1, last_arg),
            (0,),
            scalars=(0,),
            aliases={last_arg: 0},
            scratch=zonal + scratch,
            limit=56,
        )(grp_scalar, members, *sum_other, *sum_other_in, control_band, row, tables, half)
    control = control.reshape(2 * slots, 2, degrees // 2).swapaxes(1, 2)
    return recentered, control.reshape(1, 1, 2, slots, degrees)


def solution(mesh):
    bands = mesh.shape["tile"]
    waves, degrees, rows, lon = 768, 768, 48, 3072
    tables = zonal_tables(waves, lon)
    lat_table = latitude_table(degrees, bands, rows)
    placed = (
        P("grp", "lev", "tile", None),
        P("lev", "tile", None),
        P("tile", None),
        P("lev", None),
        P(),
    )
    return jax.shard_map(
        lambda *args: on_device(jnp.asarray(tables), jnp.asarray(lat_table), *args),
        mesh=mesh,
        in_specs=placed,
        out_specs=(P("grp", "lev", "tile", None), P("lev", "grp", None, "tile", None)),
        check_vma=False,
    )
```

```python
import functools
import math
import numpy as np
import jax
import jax.numpy as jnp
import ml_dtypes
from jax import lax
from jax.experimental import pallas as pl
from jax.experimental.pallas import tpu as pltpu
from jax.sharding import PartitionSpec as P

BF = jnp.bfloat16
F32 = jnp.float32
MEM = 16
ROWS = 48
SPREAD_FACTOR = 1.2
LARGE_LIMIT = 52


def split_table(table):
    high = table.astype(ml_dtypes.bfloat16)
    low = (table - high.astype(np.float64)).astype(ml_dtypes.bfloat16)
    return np.stack([high, low])


def zonal_tables(waves, lon_count):
    quarter = lon_count // 4
    columns = quarter + 128
    place = np.arange(columns)
    parts = []
    for parity in (0, 1):
        m = np.arange(parity, waves, 2)
        turn = (m[:, None] * place[None, :]) % lon_count
        angle = turn * (2.0 * math.pi / lon_count)
        for wave in (np.cos(angle), np.sin(angle)):
            wave = wave * math.sqrt(2.0 / lon_count)
            wave[:, quarter + 1 :] = 0.0
            parts.append(split_table(wave))
    return np.stack(parts)


def latitude_table(degrees, bands, rows):
    lat_count = bands * rows
    turn_index = (np.arange(degrees)[:, None] * (2 * np.arange(lat_count // 2) + 1)[None, :]) % (4 * lat_count)
    values = np.cos(turn_index * (math.pi / (2.0 * lat_count))) * math.sqrt(2.0 / lat_count)
    out = np.zeros((degrees, bands // 2, 64))
    out[:, :, :rows] = values.reshape(degrees, bands // 2, rows)
    out = out.reshape(degrees, -1)
    return np.stack([split_table(out[0::2]), split_table(out[1::2])])


class Loaded:
    def __init__(self, source, scratch, semaphores, indices, ahead=4):
        self.scratch = scratch
        self.copies = {
            index: pltpu.make_async_copy(source.at[index], scratch.at[index], semaphores.at[place])
            for place, index in enumerate(indices)
        }
        self.to_start = list(indices)
        self.to_wait = set(indices)
        for _ in range(ahead):
            self.start_next()

    def start_next(self):
        if self.to_start:
            self.copies[self.to_start.pop(0)].start()

    def __getitem__(self, index):
        if index in self.to_wait:
            while index in self.to_start:
                self.start_next()
            self.copies[index].wait()
            self.to_wait.remove(index)
            self.start_next()
        return self.scratch[index]


GROUPS = [(group, part) for group in range(4) for part in range(2)]


def halves(x):
    high = x.astype(BF)
    return high, (x - high.astype(F32)).astype(BF)


def lanes_like(x):
    return lax.broadcasted_iota(jnp.int32, x.shape, x.ndim - 1)


def flip_shift(x):
    lanes = lanes_like(x)
    return jnp.take_along_axis(x, (128 - lanes) % 128, axis=-1)


def block(x, q):
    return x[:, 128 * q : 128 * (q + 1)]


def mirrored(x, top, count, keep_first):
    out = []
    for q in range(count):
        body = flip_shift(block(x, top - 1 - q))
        first = lanes_like(body) == 0
        if q == 0 and not keep_first:
            out.append(jnp.where(first, 0.0, body))
        else:
            out.append(jnp.where(first, block(x, top - q), body))
    return jnp.concatenate(out, axis=1)


NT = (((1,), (1,)), ((), ()))
NN = (((1,), (0,)), ((), ()))
TN = (((0,), (0,)), ((), ()))


def dot(a, b, dims=NN):
    return lax.dot_general(a, b, dims, preferred_element_type=F32)


def fold(grid):
    q = grid.shape[1] // 4
    blocks = q // 128
    rows = grid.shape[0]
    zero = jnp.zeros((rows, 128), F32)
    a = grid[:, : q + 128]
    c = grid[:, 2 * q : 3 * q + 128]
    b = jnp.concatenate([mirrored(grid, 2 * blocks, blocks, False), zero], axis=1)
    d = jnp.concatenate([mirrored(grid, 4 * blocks, blocks, False), zero], axis=1)
    ac, bd, amc, bmd = a + c, b + d, a - c, b - d
    return ac + bd, ac - bd, amc - bmd, amc + bmd


def analyse(grid, table, perm):
    rows = grid.shape[0]
    pad = jnp.zeros((64 - rows, grid.shape[1] // 4 + 128), BF)
    parts = fold(grid)
    natural = []
    for parity in (0, 1):
        sums = []
        for c in (0, 1):
            high, low = halves(parts[2 * parity + c])
            both = jnp.concatenate([high, pad, low, pad], axis=0)
            if c == 1:
                both = jnp.concatenate([low, pad, high, pad], axis=0)
            acc = dot(table[2 * parity + c, 0], both, NT) + dot(table[2 * parity + c, 1], both, NT)
            sums.append(acc + pltpu.roll(acc, 64, 1))
        natural.append(jnp.where(lanes_like(sums[0]) < 64, sums[0], sums[1]))
    natural = jnp.concatenate(natural, axis=0)
    high, low = halves(natural)
    moved = dot(perm, jnp.concatenate([high, low], axis=1))
    return moved[:, :128] + moved[:, 128:]


def place_of(wave, waves):
    return wave // 2 + (wave % 2) * (waves // 2)


def to_natural(order_row):
    waves = order_row.shape[1]
    hit = lax.broadcasted_iota(jnp.int32, (waves, waves), 0) == place_of(order_row, waves)
    return hit.astype(F32).astype(BF)


def to_slots(order_row):
    waves = order_row.shape[1]
    place = jnp.broadcast_to(place_of(order_row, waves).astype(F32), (128, waves)).T
    lanes = lanes_like(place)
    hits = [(place == (lanes + first).astype(F32)).astype(F32).astype(BF) for first in range(0, waves, 128)]
    return jnp.concatenate(hits, axis=1)


def synthesise(band, table, perm_t, rows, lon):
    q = lon // 4
    blocks = q // 128
    waves = band.shape[0]
    high, low = halves(band)
    moved = dot(perm_t, jnp.concatenate([high, low], axis=1))
    natural = moved[:, :128] + moved[:, 128:]
    parts = []
    for parity in (0, 1):
        flipped = natural[parity * (waves // 2) : (parity + 1) * (waves // 2)].T
        high, low = halves(flipped)
        for c in (0, 1):
            lhs = jnp.concatenate([high[64 * c : 64 * c + 64], low[64 * c : 64 * c + 64]], axis=0)
            acc = dot(lhs, table[2 * parity + c, 0]) + dot(lhs, table[2 * parity + c, 1])
            parts.append(acc[:rows] + acc[64 : 64 + rows])
    ce, se, co, so = parts
    f1 = (ce + co + se + so)[:, :q]
    a = ce - co - se + so
    f3 = (ce - co + se - so)[:, :q]
    b = ce + co - se - so
    f2 = mirrored(a, blocks, blocks, True)
    f4 = mirrored(b, blocks, blocks, True)
    return jnp.concatenate([f1, f2, f3, f4], axis=1)


def turn(x, by):
    return pltpu.roll(x, by % 128, 1)


def pack(x):
    lanes = lanes_like(x)
    y = jnp.where(lanes < 48, x, turn(x, -16))
    k = x.shape[0] // 4
    a, b, c, d = (y[i * k : (i + 1) * k] for i in range(4))
    lanes = lanes[:k]
    return jnp.concatenate(
        [
            jnp.where(lanes < 96, a, turn(b, 96)),
            jnp.where(lanes < 64, turn(b, -32), turn(c, 64)),
            jnp.where(lanes < 32, turn(c, -64), turn(d, 32)),
        ],
        axis=0,
    )


def unpack(p):
    k = p.shape[0] // 3
    p0, p1, p2 = (p[i * k : (i + 1) * k] for i in range(3))
    lanes = lanes_like(p0)
    y = jnp.concatenate(
        [
            p0,
            jnp.where(lanes < 32, turn(p0, 32), turn(p1, 32)),
            jnp.where(lanes < 64, turn(p1, 64), turn(p2, 64)),
            turn(p2, -32),
        ],
        axis=0,
    )
    lanes = lanes_like(y)
    x = jnp.where(lanes < 48, y, turn(y, 16))
    return jnp.where((lanes < 48) | ((lanes >= 64) & (lanes < 112)), x, 0.0)


def total(x):
    return jnp.sum(jnp.sum(x, axis=0, keepdims=True), axis=1, keepdims=True)


def mark(x, values):
    rows = lax.broadcasted_iota(jnp.int32, x.shape, x.ndim - 2)
    lanes = lanes_like(x)
    for i, value in enumerate(values):
        value = value.reshape((1,) * x.ndim)
        x = jnp.where((rows == 0) & (lanes == 48 + i), value, x)
    return x


def spread(values, level):
    lanes = lax.broadcasted_iota(jnp.int32, (1, 128), 1)
    out = jnp.zeros((1, 128), F32)
    for i, value in enumerate(values):
        out = jnp.where(lanes == 8 * i + level, value, out)
    return out


def quantities(row, count):
    lanes = lanes_like(row)
    return [jnp.where(lanes < 8, turn(row, -8 * i), 0.0) for i in range(count)]


def level_sum(members_ref, level, held, semaphores):
    count = members_ref.shape[0]
    copies = [pltpu.make_async_copy(members_ref.at[k, level], held.at[k], semaphores.at[k]) for k in range(count)]
    for copy in copies:
        copy.start()

    def finish():
        acc = None
        for k in range(count):
            copies[k].wait()
            value = held[k].astype(F32)
            acc = value if acc is None else acc + value
        return acc

    return finish


PIECES = 3


def other_kernel(grp_ref, members_ref, count_ref, row_ref, table_ref, out_ref, sum_ref, held, held_table, sums_sem, table_sem):
    summed = level_sum(members_ref, 1 - grp_ref[0], held, sums_sem)
    table = Loaded(table_ref, held_table, table_sem, GROUPS)
    perm = to_slots(row_ref[...])
    acc = summed()
    sum_ref[...] = acc
    weights = count_ref[...].astype(F32) * 0.5
    out_ref[...] = pack(analyse(-weights * (acc / MEM), table, perm))


def own_kernel(grp_ref, members_ref, obs_ref, count_ref, row_ref, table_ref, sum_other_ref, out_ref, sums_ref, held, held_table, held_obs, sums_sem, table_sem, obs_sem):
    summed = level_sum(members_ref, grp_ref[0], held, sums_sem)
    obs = pltpu.make_async_copy(obs_ref.at[grp_ref[0]], held_obs, obs_sem)
    obs.start()
    table = Loaded(table_ref, held_table, table_sem, GROUPS)
    perm = to_slots(row_ref[...])
    acc = summed()
    sums_ref[0] = sum_other_ref[...]
    sums_ref[1] = acc
    weights = count_ref[...].astype(F32) * 0.5
    obs.wait()
    out_ref[...] = analyse(weights * (held_obs[...] - acc / MEM), table, perm)


def join_kernel(own_ref, packed_ref, out_ref):
    out_ref[...] = (own_ref[...] + unpack(packed_ref[...])).reshape(out_ref.shape)


LAT_GROUPS = [(parity, part) for parity in range(2) for part in range(2)]


def southern(x, rows):
    lanes = lanes_like(x)
    index = jnp.where(lanes < rows, rows - 1 - lanes, jnp.where((lanes >= 64) & (lanes < 64 + rows), 127 + rows - lanes, lanes))
    return jnp.take_along_axis(x, index, axis=-1)


def side_by_side(chunks):
    lower = lanes_like(chunks[0]) < 64
    pairs = [(chunks[k], chunks[k + 1]) for k in range(0, len(chunks), 2)]
    cos = [jnp.where(lower, x0, turn(x1, 64)) for x0, x1 in pairs]
    sin = [jnp.where(lower, turn(x0, 64), x1) for x0, x1 in pairs]
    return jnp.concatenate([jnp.concatenate(cos, axis=1), jnp.concatenate(sin, axis=1)], axis=0)


def apart(y):
    slots = y.shape[0] // 2
    out = []
    for p in range(y.shape[1] // 128):
        y0, y1 = block(y[:slots], p), block(y[slots:], p)
        lower = lanes_like(y0) < 64
        out += [jnp.where(lower, y0, turn(y1, 64)), jnp.where(lower, turn(y0, 64), y1)]
    return out


def latitude_analysis(chunks_ref, lat, rows):
    bands, slots, _ = chunks_ref.shape
    north = [chunks_ref[t] for t in range(bands // 2)]
    south = [southern(chunks_ref[bands - 1 - t], rows) for t in range(bands // 2)]
    out = []
    for parity in range(2):
        x = side_by_side([a + b if parity == 0 else a - b for a, b in zip(north, south)])
        lhs = jnp.concatenate(halves(x), axis=0)
        acc = dot(lhs, lat[parity, 0], NT) + dot(lhs, lat[parity, 1], NT)
        out.append(acc[: 2 * slots] + acc[2 * slots :])
    return jnp.concatenate(out, axis=1)


def latitude_synthesis(vector, lat, out_ref, values, rows):
    bands, slots, _ = out_ref.shape
    half = vector.shape[1] // 2
    y = []
    for parity in range(2):
        lhs = jnp.concatenate(halves(vector[:, parity * half : (parity + 1) * half]), axis=0)
        acc = dot(lhs, lat[parity, 0]) + dot(lhs, lat[parity, 1])
        y.append(acc[: 2 * slots] + acc[2 * slots :])
    for t, chunk in enumerate(apart(y[0] + y[1])):
        out_ref[t] = mark(chunk, values)
    for t, chunk in enumerate(apart(y[0] - y[1])):
        out_ref[bands - 1 - t] = mark(southern(chunk, rows), values)


def scale_of(variance, waves_col, degrees):
    slots = waves_col.shape[0]
    lane = lax.broadcasted_iota(jnp.int32, (slots, degrees), 1)
    degree = 2 * (lane % (degrees // 2)) + lane // (degrees // 2)
    scale = jnp.where(degree >= waves_col, jnp.sqrt(variance), 0.0)
    return jnp.concatenate([scale, scale], axis=0)


def latitude_first_kernel(chunks_ref, variance_ref, waves_ref, lat_ref, *refs):
    rhs_ref, out_ref, held, semaphores = refs[-4:]
    lat = Loaded(lat_ref, held, semaphores, LAT_GROUPS)
    scale = scale_of(variance_ref[...], waves_ref[...], variance_ref.shape[1])
    rhs = latitude_analysis(chunks_ref, lat, ROWS) * scale
    rhs_ref[...] = rhs
    latitude_synthesis(rhs * scale, lat, out_ref, [total(rhs * rhs)], ROWS)


def latitude_second_kernel(chunks_ref, variance_ref, waves_ref, rhs_ref, lat_ref, *refs):
    image_ref, out_ref, quotient_ref, held, semaphores = refs[-5:]
    lat = Loaded(lat_ref, held, semaphores, LAT_GROUPS)
    norm, field_norm = chunks_ref[0, 0:1, 49:50], marks(chunks_ref, 48)
    extra = jnp.where(norm > 0.0, field_norm / norm, 0.0)
    quotient_ref[...] = jnp.broadcast_to(1.0 + extra, (8, 128))
    scale = scale_of(variance_ref[...], waves_ref[...], variance_ref.shape[1])
    image = latitude_analysis(chunks_ref, lat, ROWS) * scale - extra * rhs_ref[...]
    image_ref[...] = image
    latitude_synthesis(image * scale, lat, out_ref, [], ROWS)


def marks(band_ref, lane):
    value = jnp.zeros((1, 1), F32)
    for t in range(band_ref.shape[0]):
        value = value + band_ref[t, 0:1, lane : lane + 1]
    return value


def grid_kernel(band_ref, count_ref, row_ref, table_ref, *refs):
    field_ref, out_ref, held, semaphores = refs[-4:]
    table = Loaded(table_ref, held, semaphores, GROUPS)
    bands, slots, _ = band_ref.shape
    rows, lon = count_ref.shape
    row = row_ref[...]
    field = synthesise(band_ref[...].reshape(bands * slots, 128), table, to_natural(row), rows, lon)
    field_ref[...] = field
    weighted = count_ref[...].astype(F32) * 0.5 * field
    out = analyse(weighted, table, to_slots(row)).reshape(bands, slots, 128)
    out_ref[...] = mark(out, [total(weighted * field), marks(band_ref, 48)])


def last_kernel(level_ref, band_ref, count_ref, row_ref, table_ref, field_ref, rhs_ref, image_ref, quotient_ref, *refs):
    next_ref, sums_ref, held, semaphores = refs[-4:]
    table = Loaded(table_ref, held, semaphores, GROUPS)
    bands, slots, _ = band_ref.shape
    rows, lon = count_ref.shape
    rhs, image, start = rhs_ref[...], image_ref[...], field_ref[...]
    weights = count_ref[...].astype(F32) * 0.5
    field = synthesise(band_ref[...].reshape(bands * slots, 128), table, to_natural(row_ref[...]), rows, lon)
    next_ref[...] = field
    weighted = weights * field
    row = spread(
        [
            total(rhs * rhs),
            total(weights * start * start),
            total(image * image),
            total(image * rhs),
            total(weighted * field),
            total(weighted * start),
            quotient_ref[0:1, 0:1] / bands,
        ],
        level_ref[0],
    )
    sums_ref[...] = jnp.broadcast_to(row[None], sums_ref.shape)


def combine_kernel(level_ref, sums_ref, sums_in_ref, rhs_ref, image_ref, first_ref, second_ref, control_ref, packed_ref, factors_ref):
    bands, slots, _ = first_ref.shape
    sums = sums_ref[...] + sums_in_ref[...]
    norm, field_norm, image_norm, cross, next_norm, field_cross, quotient = quantities(sums, 7)

    def over_levels(x):
        return jnp.sum(x, axis=1, keepdims=True)

    norm_all, field_all = over_levels(norm), over_levels(field_norm)
    step = norm_all / (norm_all + field_all)
    keep = 1.0 - step * quotient
    norm_next = over_levels(keep * keep * norm - 2.0 * step * keep * cross + step * step * image_norm)
    field_next = over_levels(keep * keep * field_norm - 2.0 * step * keep * field_cross + step * step * next_norm)
    mixed = over_levels(keep * (norm + field_norm) - step * (cross + field_cross))
    ratio = norm_next / norm_all
    curve = norm_next + field_next + 2.0 * ratio * mixed + ratio * ratio * (norm_all + field_all)
    step_next = norm_next / curve
    mine = lanes_like(keep) == level_ref[0]
    first = over_levels(jnp.where(mine, step + step_next * (keep + ratio), 0.0))
    second = -step_next * step
    control_ref[...] = first * rhs_ref[...] + second * image_ref[...]
    band = first * first_ref[...].reshape(bands * slots, 128) + second * second_ref[...].reshape(bands * slots, 128)
    packed_ref[...] = pack(band)
    lanes = lanes_like(sums)
    factors_ref[...] = jnp.where(lanes == 0, first, jnp.where(lanes == 1, second, 0.0))


class Recentering:
    def __init__(self, members_ref, level, sums, out_ref, scratch):
        self.near, self.near_sums, self.held, near_sem, sums_sem, self.out_sem = scratch
        self.out_ref, self.level = out_ref, level
        rows = members_ref.shape[2]
        self.cut = rows // PIECES
        self.loads = []
        for piece in range(PIECES):
            source = members_ref.at[:, level, pl.ds(piece * self.cut, self.cut)]
            self.loads.append(pltpu.make_async_copy(source, self.near.at[piece], near_sem.at[piece]))
        self.sum_loads = [
            pltpu.make_async_copy(source.at[index], self.near_sums.at[k], sums_sem.at[k]) for k, (source, index) in enumerate(sums)
        ]
        for copy in self.sum_loads + self.loads:
            copy.start()

    def run(self, increment):
        for copy in self.sum_loads:
            copy.wait()
        copies = []
        for piece in range(PIECES):
            here = slice(piece * self.cut, (piece + 1) * self.cut)
            mean = (self.near_sums[0, here] + self.near_sums[1, here]) / MEM
            offset = (mean + increment(here)) - SPREAD_FACTOR * mean
            self.loads[piece].wait()
            for k in range(self.near.shape[1]):
                self.held[piece, k] = (SPREAD_FACTOR * self.near[piece, k].astype(F32) + offset).astype(BF)
            target = self.out_ref.at[:, self.level, pl.ds(piece * self.cut, self.cut)]
            copies.append(pltpu.make_async_copy(self.held.at[piece], target, self.out_sem.at[piece]))
            copies[-1].start()
        for copy in copies:
            copy.wait()


def finish_own_kernel(grp_ref, members_ref, sums_ref, sums_in_ref, factors_ref, start_ref, next_ref, out_ref, *scratch):
    work = Recentering(members_ref, grp_ref[0], ((sums_ref, 1), (sums_in_ref, 0)), out_ref, scratch)
    first, second = factors_ref[0:1, 0:1], factors_ref[0:1, 1:2]
    work.run(lambda here: first * start_ref[here] + second * next_ref[here])


def finish_other_kernel(grp_ref, members_ref, sums_ref, sums_in_ref, packed_ref, row_ref, table_ref, half_ref, out_ref, held_table, table_sem, *scratch):
    table = Loaded(table_ref, held_table, table_sem, GROUPS)
    work = Recentering(members_ref, 1 - grp_ref[0], ((sums_ref, 0), (sums_in_ref, 1)), out_ref, scratch)
    rows, lon = members_ref.shape[2:]
    field = synthesise(unpack(packed_ref[...]), table, to_natural(row_ref[...]), rows, lon)
    work.run(lambda here: field[here])


def shape(*dims):
    return jax.ShapeDtypeStruct(dims, F32)


def call(kernel, outs, name, hbm=(), hbm_outs=(), scalars=(), aliases=None, scratch=(), limit=LARGE_LIMIT):
    def run(*args):
        def space(i, far, scalars=()):
            return pltpu.SMEM if i in scalars else pltpu.HBM if i in far else pltpu.VMEM

        return pl.pallas_call(
            kernel,
            out_shape=outs,
            in_specs=[pl.BlockSpec(memory_space=space(i, hbm, scalars)) for i in range(len(args))],
            out_specs=[pl.BlockSpec(memory_space=space(o, hbm_outs)) for o in range(len(outs))],
            input_output_aliases=aliases or {},
            scratch_shapes=scratch,
            compiler_params=pltpu.CompilerParams(vmem_limit_bytes=limit * 2**20),
            cost_estimate=pl.CostEstimate(flops=1, bytes_accessed=1, transcendentals=0),
            name=name,
        )(*args)

    return run


def on_device(tables, lat_table, members, obs_value, obs_count, variance, wave_order):
    grp = lax.axis_index("grp")
    bands = lax.axis_size("tile")
    levels = lax.axis_size("lev")
    mem, _, rows, lon = members.shape
    waves = wave_order.shape[0]
    slots = waves // bands
    degrees = variance.shape[1]
    swap = [(0, 1), (1, 0)]
    own_waves = lax.dynamic_slice_in_dim(wave_order, lax.axis_index("tile") * slots, slots, 0)[:, None]
    own_variance = lax.dynamic_index_in_dim(variance, grp, 0, keepdims=False)
    own_variance = own_variance.reshape(degrees // 2, 2).T.reshape(1, degrees)
    row = wave_order[None, :]
    grp_scalar = grp[None].astype(jnp.int32)

    chunk = shape(bands, slots, 128)
    packed = shape(waves * 3 // 4, 128)
    field = shape(rows, lon)
    vector = shape(2 * slots, degrees)
    small = shape(8, 128)
    dma = pltpu.SemaphoreType.DMA
    zonal = [pltpu.VMEM(tables.shape, BF), dma((len(GROUPS),))]
    latitude = [pltpu.VMEM(lat_table.shape, BF), dma((len(LAT_GROUPS),))]
    level = pltpu.VMEM((mem, rows, lon), BF)
    cut = rows // PIECES
    level_scalar = (2 * lax.axis_index("lev") + grp)[None].astype(jnp.int32)

    def trade(array):
        return lax.ppermute(array, "grp", swap)

    with jax.named_scope("start"):
        coeffs_other, sum_other = call(
            other_kernel, [packed, field], "other", (1, 4), scalars=(0,), scratch=[level, zonal[0], dma((mem,)), zonal[1]]
        )(grp_scalar, members, obs_count, row, tables)
        coeffs_in = trade(coeffs_other)
        coeffs_own, sums = call(
            own_kernel,
            [shape(waves, 128), shape(2, rows, lon)],
            "own",
            (1, 2, 5),
            scalars=(0,),
            scratch=[level, zonal[0], pltpu.VMEM((rows, lon), F32), dma((mem,)), zonal[1], dma],
        )(grp_scalar, members, obs_value, obs_count, row, tables, sum_other)
        (coeffs,) = call(join_kernel, [chunk], "join")(coeffs_own, coeffs_in)
        sums_in = trade(sums)

    def exchange(chunks):
        return lax.all_to_all(chunks, "tile", 0, 0, tiled=True)

    with jax.named_scope("solve"):
        rhs, lat_values = call(latitude_first_kernel, [vector, chunk], "lat1", (3,), scratch=latitude)(
            exchange(coeffs), own_variance, own_waves, lat_table
        )
        band_first = exchange(lat_values)
        field_own, coeffs = call(grid_kernel, [field, chunk], "grid", (3,), scratch=zonal)(
            band_first, obs_count, row, tables
        )
        image, lat_values, quotient = call(latitude_second_kernel, [vector, chunk, small], "lat2", (4, 5), scratch=latitude)(
            exchange(coeffs), own_variance, own_waves, rhs, lat_table, sums_in
        )
        band_second = exchange(lat_values)
        sum_row = jax.ShapeDtypeStruct((bands, 1, 128), F32)
        next_own, scalars = call(last_kernel, [field, sum_row], "last", (4,), scalars=(0,), scratch=zonal)(
            level_scalar, band_second, obs_count, row, tables, field_own, rhs, image, quotient
        )
        scalars = jnp.sum(exchange(scalars), axis=0)
        for step in (1, 2):
            scalars = scalars + lax.ppermute(scalars, "lev", [(i, i ^ step) for i in range(levels)])

    with jax.named_scope("finish"):
        control, control_band, factors = call(combine_kernel, [vector, packed, shape(1, 128)], "combine", scalars=(0,), limit=16)(
            level_scalar, scalars, trade(scalars), rhs, image, band_first, band_second
        )
        control_band = trade(control_band)
        near = pltpu.VMEM((PIECES, mem, cut, lon), BF)
        scratch = [near, pltpu.VMEM((2, rows, lon), F32), near, dma((PIECES,)), dma((2,)), dma((PIECES,))]
        whole_out = jax.ShapeDtypeStruct(members.shape, BF)
        (half,) = call(finish_own_kernel, [whole_out], "finish_own", (1, 2, 3), (0,), scalars=(0,), scratch=scratch)(
            grp_scalar, members, sums, sums_in, factors, field_own, next_own
        )
        (recentered,) = call(
            finish_other_kernel, [whole_out], "finish_other", (1, 2, 3, 6, 7), (0,), scalars=(0,), aliases={7: 0}, scratch=zonal + scratch
        )(grp_scalar, members, sums, sums_in, control_band, row, tables, half)
    control = control.reshape(2 * slots, 2, degrees // 2).swapaxes(1, 2)
    return recentered, control.reshape(1, 1, 2, slots, degrees)


def solution(mesh):
    bands = mesh.shape["tile"]
    waves, degrees, rows, lon = 768, 768, 48, 3072
    tables = zonal_tables(waves, lon)
    lat_table = latitude_table(degrees, bands, rows)
    placed = (
        P("grp", "lev", "tile", None),
        P("lev", "tile", None),
        P("tile", None),
        P("lev", None),
        P(),
    )
    return jax.shard_map(
        lambda *args: on_device(jnp.asarray(tables), jnp.asarray(lat_table), *args),
        mesh=mesh,
        in_specs=placed,
        out_specs=(P("grp", "lev", "tile", None), P("lev", "grp", None, "tile", None)),
        check_vma=False,
    )
```

```python
import functools
import math
import numpy as np
import jax
import jax.numpy as jnp
import ml_dtypes
from jax import lax
from jax.experimental import pallas as pl
from jax.experimental.pallas import tpu as pltpu
from jax.sharding import PartitionSpec as P

BF = jnp.bfloat16
F32 = jnp.float32
MEM = 16
ROWS = 48
SPREAD_FACTOR = 1.2
LARGE_LIMIT = 52


def split_table(table):
    high = table.astype(ml_dtypes.bfloat16)
    low = (table - high.astype(np.float64)).astype(ml_dtypes.bfloat16)
    return np.stack([high, low])


def zonal_tables(waves, lon_count):
    quarter = lon_count // 4
    columns = quarter + 128
    place = np.arange(columns)
    parts = []
    for parity in (0, 1):
        m = np.arange(parity, waves, 2)
        turn = (m[:, None] * place[None, :]) % lon_count
        angle = turn * (2.0 * math.pi / lon_count)
        for wave in (np.cos(angle), np.sin(angle)):
            wave = wave * math.sqrt(2.0 / lon_count)
            wave[:, quarter + 1 :] = 0.0
            parts.append(split_table(wave))
    return np.stack(parts)


def latitude_table(degrees, bands, rows):
    lat_count = bands * rows
    turn_index = (np.arange(degrees)[:, None] * (2 * np.arange(lat_count // 2) + 1)[None, :]) % (4 * lat_count)
    values = np.cos(turn_index * (math.pi / (2.0 * lat_count))) * math.sqrt(2.0 / lat_count)
    out = np.zeros((degrees, bands // 2, 64))
    out[:, :, :rows] = values.reshape(degrees, bands // 2, rows)
    out = out.reshape(degrees, -1)
    return np.stack([split_table(out[0::2]), split_table(out[1::2])])


class Loaded:
    def __init__(self, source, scratch, semaphores, indices, ahead=4):
        self.scratch = scratch
        self.copies = {
            index: pltpu.make_async_copy(source.at[index], scratch.at[index], semaphores.at[place])
            for place, index in enumerate(indices)
        }
        self.to_start = list(indices)
        self.to_wait = set(indices)
        for _ in range(ahead):
            self.start_next()

    def start_next(self):
        if self.to_start:
            self.copies[self.to_start.pop(0)].start()

    def __getitem__(self, index):
        if index in self.to_wait:
            while index in self.to_start:
                self.start_next()
            self.copies[index].wait()
            self.to_wait.remove(index)
            self.start_next()
        return self.scratch[index]


GROUPS = [(group, part) for group in range(4) for part in range(2)]


def halves(x):
    high = x.astype(BF)
    return high, (x - high.astype(F32)).astype(BF)


def lanes_like(x):
    return lax.broadcasted_iota(jnp.int32, x.shape, x.ndim - 1)


def flip_shift(x):
    lanes = lanes_like(x)
    return jnp.take_along_axis(x, (128 - lanes) % 128, axis=-1)


def block(x, q):
    return x[:, 128 * q : 128 * (q + 1)]


def mirrored(x, top, count, keep_first):
    out = []
    for q in range(count):
        body = flip_shift(block(x, top - 1 - q))
        first = lanes_like(body) == 0
        if q == 0 and not keep_first:
            out.append(jnp.where(first, 0.0, body))
        else:
            out.append(jnp.where(first, block(x, top - q), body))
    return jnp.concatenate(out, axis=1)


NT = (((1,), (1,)), ((), ()))
NN = (((1,), (0,)), ((), ()))
TN = (((0,), (0,)), ((), ()))


def dot(a, b, dims=NN):
    return lax.dot_general(a, b, dims, preferred_element_type=F32)


def fold(grid):
    q = grid.shape[1] // 4
    blocks = q // 128
    rows = grid.shape[0]
    zero = jnp.zeros((rows, 128), F32)
    a = grid[:, : q + 128]
    c = grid[:, 2 * q : 3 * q + 128]
    b = jnp.concatenate([mirrored(grid, 2 * blocks, blocks, False), zero], axis=1)
    d = jnp.concatenate([mirrored(grid, 4 * blocks, blocks, False), zero], axis=1)
    ac, bd, amc, bmd = a + c, b + d, a - c, b - d
    return ac + bd, ac - bd, amc - bmd, amc + bmd


def analyse(grid, table, perm):
    rows = grid.shape[0]
    pad = jnp.zeros((64 - rows, grid.shape[1] // 4 + 128), BF)
    parts = fold(grid)
    natural = []
    for parity in (0, 1):
        sums = []
        for c in (0, 1):
            high, low = halves(parts[2 * parity + c])
            both = jnp.concatenate([high, pad, low, pad], axis=0)
            if c == 1:
                both = jnp.concatenate([low, pad, high, pad], axis=0)
            acc = dot(table[2 * parity + c, 0], both, NT) + dot(table[2 * parity + c, 1], both, NT)
            sums.append(acc + pltpu.roll(acc, 64, 1))
        natural.append(jnp.where(lanes_like(sums[0]) < 64, sums[0], sums[1]))
    natural = jnp.concatenate(natural, axis=0)
    high, low = halves(natural)
    moved = dot(perm, jnp.concatenate([high, low], axis=1))
    return moved[:, :128] + moved[:, 128:]


def place_of(wave, waves):
    return wave // 2 + (wave % 2) * (waves // 2)


def to_natural(order_row):
    waves = order_row.shape[1]
    hit = lax.broadcasted_iota(jnp.int32, (waves, waves), 0) == place_of(order_row, waves)
    return hit.astype(F32).astype(BF)


def to_slots(order_row):
    waves = order_row.shape[1]
    place = jnp.broadcast_to(place_of(order_row, waves).astype(F32), (128, waves)).T
    lanes = lanes_like(place)
    hits = [(place == (lanes + first).astype(F32)).astype(F32).astype(BF) for first in range(0, waves, 128)]
    return jnp.concatenate(hits, axis=1)


def synthesise(band, table, perm_t, rows, lon):
    q = lon // 4
    blocks = q // 128
    waves = band.shape[0]
    high, low = halves(band)
    moved = dot(perm_t, jnp.concatenate([high, low], axis=1))
    natural = moved[:, :128] + moved[:, 128:]
    parts = []
    for parity in (0, 1):
        flipped = natural[parity * (waves // 2) : (parity + 1) * (waves // 2)].T
        high, low = halves(flipped)
        for c in (0, 1):
            lhs = jnp.concatenate([high[64 * c : 64 * c + 64], low[64 * c : 64 * c + 64]], axis=0)
            acc = dot(lhs, table[2 * parity + c, 0]) + dot(lhs, table[2 * parity + c, 1])
            parts.append(acc[:rows] + acc[64 : 64 + rows])
    ce, se, co, so = parts
    f1 = (ce + co + se + so)[:, :q]
    a = ce - co - se + so
    f3 = (ce - co + se - so)[:, :q]
    b = ce + co - se - so
    f2 = mirrored(a, blocks, blocks, True)
    f4 = mirrored(b, blocks, blocks, True)
    return jnp.concatenate([f1, f2, f3, f4], axis=1)


def turn(x, by):
    return pltpu.roll(x, by % 128, 1)


def pack(x):
    lanes = lanes_like(x)
    y = jnp.where(lanes < 48, x, turn(x, -16))
    k = x.shape[0] // 4
    a, b, c, d = (y[i * k : (i + 1) * k] for i in range(4))
    lanes = lanes[:k]
    return jnp.concatenate(
        [
            jnp.where(lanes < 96, a, turn(b, 96)),
            jnp.where(lanes < 64, turn(b, -32), turn(c, 64)),
            jnp.where(lanes < 32, turn(c, -64), turn(d, 32)),
        ],
        axis=0,
    )


def unpack(p):
    k = p.shape[0] // 3
    p0, p1, p2 = (p[i * k : (i + 1) * k] for i in range(3))
    lanes = lanes_like(p0)
    y = jnp.concatenate(
        [
            p0,
            jnp.where(lanes < 32, turn(p0, 32), turn(p1, 32)),
            jnp.where(lanes < 64, turn(p1, 64), turn(p2, 64)),
            turn(p2, -32),
        ],
        axis=0,
    )
    lanes = lanes_like(y)
    x = jnp.where(lanes < 48, y, turn(y, 16))
    return jnp.where((lanes < 48) | ((lanes >= 64) & (lanes < 112)), x, 0.0)


def total(x):
    return jnp.sum(jnp.sum(x, axis=0, keepdims=True), axis=1, keepdims=True)


def mark(x, values):
    rows = lax.broadcasted_iota(jnp.int32, x.shape, x.ndim - 2)
    lanes = lanes_like(x)
    for i, value in enumerate(values):
        value = value.reshape((1,) * x.ndim)
        x = jnp.where((rows == 0) & (lanes == 48 + i), value, x)
    return x


def spread(values, level):
    lanes = lax.broadcasted_iota(jnp.int32, (1, 128), 1)
    out = jnp.zeros((1, 128), F32)
    for i, value in enumerate(values):
        out = jnp.where(lanes == 8 * i + level, value, out)
    return out


def quantities(row, count):
    lanes = lanes_like(row)
    return [jnp.where(lanes < 8, turn(row, -8 * i), 0.0) for i in range(count)]


def level_sum(members_ref, level, held, semaphores):
    count = members_ref.shape[0]
    copies = [pltpu.make_async_copy(members_ref.at[k, level], held.at[k], semaphores.at[k]) for k in range(count)]
    for copy in copies:
        copy.start()

    def finish():
        acc = None
        for k in range(count):
            copies[k].wait()
            value = held[k].astype(F32)
            acc = value if acc is None else acc + value
        return acc

    return finish


PIECES = 3


def other_kernel(grp_ref, members_ref, count_ref, order_ref, table_ref, out_ref, sum_ref, held, held_table, held_count, sums_sem, table_sem, count_sem):
    summed = level_sum(members_ref, 1 - grp_ref[0], held, sums_sem)
    count = pltpu.make_async_copy(count_ref, held_count, count_sem)
    count.start()
    table = Loaded(table_ref, held_table, table_sem, GROUPS)
    perm = to_slots(order_ref[...].reshape(1, order_ref.shape[0]))
    acc = summed()
    sum_ref[...] = acc
    count.wait()
    weights = held_count[...].astype(F32) * 0.5
    out_ref[...] = pack(analyse(-weights * (acc / MEM), table, perm))


def own_kernel(grp_ref, members_ref, obs_ref, count_ref, row_ref, table_ref, sum_other_ref, out_ref, sums_ref, held, held_table, held_obs, sums_sem, table_sem, obs_sem):
    summed = level_sum(members_ref, grp_ref[0], held, sums_sem)
    obs = pltpu.make_async_copy(obs_ref.at[grp_ref[0]], held_obs, obs_sem)
    obs.start()
    table = Loaded(table_ref, held_table, table_sem, GROUPS)
    perm = to_slots(row_ref[...])
    acc = summed()
    sums_ref[0] = sum_other_ref[...]
    sums_ref[1] = acc
    weights = count_ref[...].astype(F32) * 0.5
    obs.wait()
    out_ref[...] = analyse(weights * (held_obs[...] - acc / MEM), table, perm)


def join_kernel(own_ref, packed_ref, out_ref):
    out_ref[...] = (own_ref[...] + unpack(packed_ref[...])).reshape(out_ref.shape)


LAT_GROUPS = [(parity, part) for parity in range(2) for part in range(2)]


def southern(x, rows):
    lanes = lanes_like(x)
    index = jnp.where(lanes < rows, rows - 1 - lanes, jnp.where((lanes >= 64) & (lanes < 64 + rows), 127 + rows - lanes, lanes))
    return jnp.take_along_axis(x, index, axis=-1)


def side_by_side(chunks):
    lower = lanes_like(chunks[0]) < 64
    pairs = [(chunks[k], chunks[k + 1]) for k in range(0, len(chunks), 2)]
    cos = [jnp.where(lower, x0, turn(x1, 64)) for x0, x1 in pairs]
    sin = [jnp.where(lower, turn(x0, 64), x1) for x0, x1 in pairs]
    return jnp.concatenate([jnp.concatenate(cos, axis=1), jnp.concatenate(sin, axis=1)], axis=0)


def apart(y):
    slots = y.shape[0] // 2
    out = []
    for p in range(y.shape[1] // 128):
        y0, y1 = block(y[:slots], p), block(y[slots:], p)
        lower = lanes_like(y0) < 64
        out += [jnp.where(lower, y0, turn(y1, 64)), jnp.where(lower, turn(y0, 64), y1)]
    return out


def latitude_analysis(chunks_ref, lat, rows):
    bands, slots, _ = chunks_ref.shape
    north = [chunks_ref[t] for t in range(bands // 2)]
    south = [southern(chunks_ref[bands - 1 - t], rows) for t in range(bands // 2)]
    out = []
    for parity in range(2):
        x = side_by_side([a + b if parity == 0 else a - b for a, b in zip(north, south)])
        lhs = jnp.concatenate(halves(x), axis=0)
        acc = dot(lhs, lat[parity, 0], NT) + dot(lhs, lat[parity, 1], NT)
        out.append(acc[: 2 * slots] + acc[2 * slots :])
    return jnp.concatenate(out, axis=1)


def latitude_synthesis(vector, lat, out_ref, values, rows):
    bands, slots, _ = out_ref.shape
    half = vector.shape[1] // 2
    y = []
    for parity in range(2):
        lhs = jnp.concatenate(halves(vector[:, parity * half : (parity + 1) * half]), axis=0)
        acc = dot(lhs, lat[parity, 0]) + dot(lhs, lat[parity, 1])
        y.append(acc[: 2 * slots] + acc[2 * slots :])
    for t, chunk in enumerate(apart(y[0] + y[1])):
        out_ref[t] = mark(chunk, values)
    for t, chunk in enumerate(apart(y[0] - y[1])):
        out_ref[bands - 1 - t] = mark(southern(chunk, rows), values)


def scale_of(variance, waves_col, degrees):
    slots = waves_col.shape[0]
    lane = lax.broadcasted_iota(jnp.int32, (slots, degrees), 1)
    degree = 2 * (lane % (degrees // 2)) + lane // (degrees // 2)
    scale = jnp.where(degree >= waves_col, jnp.sqrt(variance), 0.0)
    return jnp.concatenate([scale, scale], axis=0)


def latitude_first_kernel(chunks_ref, variance_ref, waves_ref, lat_ref, *refs):
    rhs_ref, out_ref, held, semaphores = refs[-4:]
    lat = Loaded(lat_ref, held, semaphores, LAT_GROUPS)
    scale = scale_of(variance_ref[...], waves_ref[...], variance_ref.shape[1])
    rhs = latitude_analysis(chunks_ref, lat, ROWS) * scale
    rhs_ref[...] = rhs
    latitude_synthesis(rhs * scale, lat, out_ref, [total(rhs * rhs)], ROWS)


def latitude_second_kernel(chunks_ref, variance_ref, waves_ref, rhs_ref, lat_ref, *refs):
    image_ref, out_ref, quotient_ref, held, semaphores = refs[-5:]
    lat = Loaded(lat_ref, held, semaphores, LAT_GROUPS)
    norm, field_norm = chunks_ref[0, 0:1, 49:50], marks(chunks_ref, 48)
    extra = jnp.where(norm > 0.0, field_norm / norm, 0.0)
    quotient_ref[...] = jnp.broadcast_to(1.0 + extra, (8, 128))
    scale = scale_of(variance_ref[...], waves_ref[...], variance_ref.shape[1])
    image = latitude_analysis(chunks_ref, lat, ROWS) * scale - extra * rhs_ref[...]
    image_ref[...] = image
    latitude_synthesis(image * scale, lat, out_ref, [], ROWS)


def marks(band_ref, lane):
    value = jnp.zeros((1, 1), F32)
    for t in range(band_ref.shape[0]):
        value = value + band_ref[t, 0:1, lane : lane + 1]
    return value


def grid_kernel(band_ref, count_ref, row_ref, table_ref, *refs):
    field_ref, out_ref, held, semaphores = refs[-4:]
    table = Loaded(table_ref, held, semaphores, GROUPS)
    bands, slots, _ = band_ref.shape
    rows, lon = count_ref.shape
    row = row_ref[...]
    field = synthesise(band_ref[...].reshape(bands * slots, 128), table, to_natural(row), rows, lon)
    field_ref[...] = field
    weighted = count_ref[...].astype(F32) * 0.5 * field
    out = analyse(weighted, table, to_slots(row)).reshape(bands, slots, 128)
    out_ref[...] = mark(out, [total(weighted * field), marks(band_ref, 48)])


def last_kernel(level_ref, band_ref, count_ref, row_ref, table_ref, field_ref, rhs_ref, image_ref, quotient_ref, *refs):
    next_ref, sums_ref, held, semaphores = refs[-4:]
    table = Loaded(table_ref, held, semaphores, GROUPS)
    bands, slots, _ = band_ref.shape
    rows, lon = count_ref.shape
    rhs, image, start = rhs_ref[...], image_ref[...], field_ref[...]
    weights = count_ref[...].astype(F32) * 0.5
    field = synthesise(band_ref[...].reshape(bands * slots, 128), table, to_natural(row_ref[...]), rows, lon)
    next_ref[...] = field
    weighted = weights * field
    row = spread(
        [
            total(rhs * rhs),
            total(weights * start * start),
            total(image * image),
            total(image * rhs),
            total(weighted * field),
            total(weighted * start),
            quotient_ref[0:1, 0:1] / bands,
        ],
        level_ref[0],
    )
    sums_ref[...] = jnp.broadcast_to(row[None], sums_ref.shape)


def combine_kernel(level_ref, sums_ref, sums_in_ref, rhs_ref, image_ref, first_ref, second_ref, control_ref, packed_ref, factors_ref):
    bands, slots, _ = first_ref.shape
    sums = sums_ref[...] + sums_in_ref[...]
    norm, field_norm, image_norm, cross, next_norm, field_cross, quotient = quantities(sums, 7)

    def over_levels(x):
        return jnp.sum(x, axis=1, keepdims=True)

    norm_all, field_all = over_levels(norm), over_levels(field_norm)
    step = norm_all / (norm_all + field_all)
    keep = 1.0 - step * quotient
    norm_next = over_levels(keep * keep * norm - 2.0 * step * keep * cross + step * step * image_norm)
    field_next = over_levels(keep * keep * field_norm - 2.0 * step * keep * field_cross + step * step * next_norm)
    mixed = over_levels(keep * (norm + field_norm) - step * (cross + field_cross))
    ratio = norm_next / norm_all
    curve = norm_next + field_next + 2.0 * ratio * mixed + ratio * ratio * (norm_all + field_all)
    step_next = norm_next / curve
    mine = lanes_like(keep) == level_ref[0]
    first = over_levels(jnp.where(mine, step + step_next * (keep + ratio), 0.0))
    second = -step_next * step
    control_ref[...] = first * rhs_ref[...] + second * image_ref[...]
    band = first * first_ref[...].reshape(bands * slots, 128) + second * second_ref[...].reshape(bands * slots, 128)
    packed_ref[...] = pack(band)
    lanes = lanes_like(sums)
    factors_ref[...] = jnp.where(lanes == 0, first, jnp.where(lanes == 1, second, 0.0))


class Recentering:
    def __init__(self, members_ref, level, sums, out_ref, scratch):
        self.near, self.near_sums, self.held, near_sem, sums_sem, self.out_sem = scratch
        self.out_ref, self.level = out_ref, level
        rows = members_ref.shape[2]
        self.cut = rows // PIECES
        self.loads = []
        for piece in range(PIECES):
            source = members_ref.at[:, level, pl.ds(piece * self.cut, self.cut)]
            self.loads.append(pltpu.make_async_copy(source, self.near.at[piece], near_sem.at[piece]))
        self.sum_loads = [
            pltpu.make_async_copy(source.at[index], self.near_sums.at[k], sums_sem.at[k]) for k, (source, index) in enumerate(sums)
        ]
        for copy in self.sum_loads + self.loads:
            copy.start()

    def run(self, increment):
        for copy in self.sum_loads:
            copy.wait()
        copies = []
        for piece in range(PIECES):
            here = slice(piece * self.cut, (piece + 1) * self.cut)
            mean = (self.near_sums[0, here] + self.near_sums[1, here]) / MEM
            offset = (mean + increment(here)) - SPREAD_FACTOR * mean
            self.loads[piece].wait()
            for k in range(self.near.shape[1]):
                self.held[piece, k] = (SPREAD_FACTOR * self.near[piece, k].astype(F32) + offset).astype(BF)
            target = self.out_ref.at[:, self.level, pl.ds(piece * self.cut, self.cut)]
            copies.append(pltpu.make_async_copy(self.held.at[piece], target, self.out_sem.at[piece]))
            copies[-1].start()
        for copy in copies:
            copy.wait()


def finish_own_kernel(grp_ref, members_ref, sums_ref, sums_in_ref, factors_ref, start_ref, next_ref, out_ref, *scratch):
    work = Recentering(members_ref, grp_ref[0], ((sums_ref, 1), (sums_in_ref, 0)), out_ref, scratch)
    first, second = factors_ref[0:1, 0:1], factors_ref[0:1, 1:2]
    work.run(lambda here: first * start_ref[here] + second * next_ref[here])


def finish_other_kernel(grp_ref, members_ref, sums_ref, sums_in_ref, packed_ref, row_ref, table_ref, half_ref, out_ref, held_table, table_sem, *scratch):
    table = Loaded(table_ref, held_table, table_sem, GROUPS, ahead=len(GROUPS))
    work = Recentering(members_ref, 1 - grp_ref[0], ((sums_ref, 0), (sums_in_ref, 1)), out_ref, scratch)
    rows, lon = members_ref.shape[2:]
    field = synthesise(unpack(packed_ref[...]), table, to_natural(row_ref[...]), rows, lon)
    work.run(lambda here: field[here])


def shape(*dims):
    return jax.ShapeDtypeStruct(dims, F32)


def call(kernel, outs, name, hbm=(), hbm_outs=(), scalars=(), aliases=None, scratch=(), limit=LARGE_LIMIT):
    def run(*args):
        def space(i, far, scalars=()):
            return pltpu.SMEM if i in scalars else pltpu.HBM if i in far else pltpu.VMEM

        return pl.pallas_call(
            kernel,
            out_shape=outs,
            in_specs=[pl.BlockSpec(memory_space=space(i, hbm, scalars)) for i in range(len(args))],
            out_specs=[pl.BlockSpec(memory_space=space(o, hbm_outs)) for o in range(len(outs))],
            input_output_aliases=aliases or {},
            scratch_shapes=scratch,
            compiler_params=pltpu.CompilerParams(vmem_limit_bytes=limit * 2**20),
            cost_estimate=pl.CostEstimate(flops=1, bytes_accessed=1, transcendentals=0),
            name=name,
        )(*args)

    return run


def on_device(tables, lat_table, members, obs_value, obs_count, variance, wave_order):
    grp = lax.axis_index("grp")
    bands = lax.axis_size("tile")
    levels = lax.axis_size("lev")
    mem, _, rows, lon = members.shape
    waves = wave_order.shape[0]
    slots = waves // bands
    degrees = variance.shape[1]
    swap = [(0, 1), (1, 0)]
    own_waves = lax.dynamic_slice_in_dim(wave_order, lax.axis_index("tile") * slots, slots, 0)[:, None]
    own_variance = lax.dynamic_index_in_dim(variance, grp, 0, keepdims=False)
    own_variance = own_variance.reshape(degrees // 2, 2).T.reshape(1, degrees)
    row = wave_order[None, :]
    grp_scalar = grp[None].astype(jnp.int32)

    chunk = shape(bands, slots, 128)
    packed = shape(waves * 3 // 4, 128)
    field = shape(rows, lon)
    vector = shape(2 * slots, degrees)
    small = shape(8, 128)
    dma = pltpu.SemaphoreType.DMA
    zonal = [pltpu.VMEM(tables.shape, BF), dma((len(GROUPS),))]
    latitude = [pltpu.VMEM(lat_table.shape, BF), dma((len(LAT_GROUPS),))]
    level = pltpu.VMEM((mem, rows, lon), BF)
    cut = rows // PIECES
    level_scalar = (2 * lax.axis_index("lev") + grp)[None].astype(jnp.int32)

    def trade(array):
        return lax.ppermute(array, "grp", swap)

    with jax.named_scope("start"):
        coeffs_other, sum_other = call(
            other_kernel, [packed, field], "other", (1, 2, 4), scalars=(0,), scratch=[level, zonal[0], pltpu.VMEM((rows, lon), jnp.int32), dma((mem,)), zonal[1], dma]
        )(grp_scalar, members, obs_count, wave_order, tables)
        coeffs_in = trade(coeffs_other)
        coeffs_own, sums = call(
            own_kernel,
            [shape(waves, 128), shape(2, rows, lon)],
            "own",
            (1, 2, 5),
            scalars=(0,),
            scratch=[level, zonal[0], pltpu.VMEM((rows, lon), F32), dma((mem,)), zonal[1], dma],
        )(grp_scalar, members, obs_value, obs_count, row, tables, sum_other)
        (coeffs,) = call(join_kernel, [chunk], "join")(coeffs_own, coeffs_in)
        sums_in = trade(sums)

    def exchange(chunks):
        return lax.all_to_all(chunks, "tile", 0, 0, tiled=True)

    with jax.named_scope("solve"):
        rhs, lat_values = call(latitude_first_kernel, [vector, chunk], "lat1", (3,), scratch=latitude)(
            exchange(coeffs), own_variance, own_waves, lat_table
        )
        band_first = exchange(lat_values)
        field_own, coeffs = call(grid_kernel, [field, chunk], "grid", (3,), scratch=zonal)(
            band_first, obs_count, row, tables
        )
        image, lat_values, quotient = call(latitude_second_kernel, [vector, chunk, small], "lat2", (4, 5), scratch=latitude)(
            exchange(coeffs), own_variance, own_waves, rhs, lat_table, sums_in
        )
        band_second = exchange(lat_values)
        sum_row = jax.ShapeDtypeStruct((bands, 1, 128), F32)
        next_own, scalars = call(last_kernel, [field, sum_row], "last", (4,), scalars=(0,), scratch=zonal)(
            level_scalar, band_second, obs_count, row, tables, field_own, rhs, image, quotient
        )
        scalars = jnp.sum(exchange(scalars), axis=0)
        for step in (1, 2):
            scalars = scalars + lax.ppermute(scalars, "lev", [(i, i ^ step) for i in range(levels)])

    with jax.named_scope("finish"):
        control, control_band, factors = call(combine_kernel, [vector, packed, shape(1, 128)], "combine", scalars=(0,), limit=16)(
            level_scalar, scalars, trade(scalars), rhs, image, band_first, band_second
        )
        control_band = trade(control_band)
        near = pltpu.VMEM((PIECES, mem, cut, lon), BF)
        scratch = [near, pltpu.VMEM((2, rows, lon), F32), near, dma((PIECES,)), dma((2,)), dma((PIECES,))]
        whole_out = jax.ShapeDtypeStruct(members.shape, BF)
        (half,) = call(finish_own_kernel, [whole_out], "finish_own", (1, 2, 3), (0,), scalars=(0,), scratch=scratch)(
            grp_scalar, members, sums, sums_in, factors, field_own, next_own
        )
        (recentered,) = call(
            finish_other_kernel, [whole_out], "finish_other", (1, 2, 3, 6, 7), (0,), scalars=(0,), aliases={7: 0}, scratch=zonal + scratch
        )(grp_scalar, members, sums, sums_in, control_band, row, tables, half)
    control = control.reshape(2 * slots, 2, degrees // 2).swapaxes(1, 2)
    return recentered, control.reshape(1, 1, 2, slots, degrees)


def solution(mesh):
    bands = mesh.shape["tile"]
    waves, degrees, rows, lon = 768, 768, 48, 3072
    tables = zonal_tables(waves, lon)
    lat_table = latitude_table(degrees, bands, rows)
    placed = (
        P("grp", "lev", "tile", None),
        P("lev", "tile", None),
        P("tile", None),
        P("lev", None),
        P(),
    )
    return jax.shard_map(
        lambda *args: on_device(jnp.asarray(tables), jnp.asarray(lat_table), *args),
        mesh=mesh,
        in_specs=placed,
        out_specs=(P("grp", "lev", "tile", None), P("lev", "grp", None, "tile", None)),
        check_vma=False,
    )
```

```python
import functools
import math
import numpy as np
import jax
import jax.numpy as jnp
import ml_dtypes
from jax import lax
from jax.experimental import pallas as pl
from jax.experimental.pallas import tpu as pltpu
from jax.sharding import PartitionSpec as P

BF = jnp.bfloat16
F32 = jnp.float32
MEM = 16
ROWS = 48
SPREAD_FACTOR = 1.2
LARGE_LIMIT = 52


def split_table(table):
    high = table.astype(ml_dtypes.bfloat16)
    low = (table - high.astype(np.float64)).astype(ml_dtypes.bfloat16)
    return np.stack([high, low])


def zonal_tables(waves, lon_count):
    quarter = lon_count // 4
    columns = quarter + 128
    place = np.arange(columns)
    parts = []
    for parity in (0, 1):
        m = np.arange(parity, waves, 2)
        turn = (m[:, None] * place[None, :]) % lon_count
        angle = turn * (2.0 * math.pi / lon_count)
        for wave in (np.cos(angle), np.sin(angle)):
            wave = wave * math.sqrt(2.0 / lon_count)
            wave[:, quarter + 1 :] = 0.0
            parts.append(split_table(wave))
    return np.stack(parts)


def latitude_table(degrees, bands, rows):
    lat_count = bands * rows
    turn_index = (np.arange(degrees)[:, None] * (2 * np.arange(lat_count // 2) + 1)[None, :]) % (4 * lat_count)
    values = np.cos(turn_index * (math.pi / (2.0 * lat_count))) * math.sqrt(2.0 / lat_count)
    out = np.zeros((degrees, bands // 2, 64))
    out[:, :, :rows] = values.reshape(degrees, bands // 2, rows)
    out = out.reshape(degrees, -1)
    return np.stack([split_table(out[0::2]), split_table(out[1::2])])


class Loaded:
    def __init__(self, source, scratch, semaphores, indices, ahead=4):
        self.scratch = scratch
        self.copies = {
            index: pltpu.make_async_copy(source.at[index], scratch.at[index], semaphores.at[place])
            for place, index in enumerate(indices)
        }
        self.to_start = list(indices)
        self.to_wait = set(indices)
        for _ in range(ahead):
            self.start_next()

    def start_next(self):
        if self.to_start:
            self.copies[self.to_start.pop(0)].start()

    def __getitem__(self, index):
        if index in self.to_wait:
            while index in self.to_start:
                self.start_next()
            self.copies[index].wait()
            self.to_wait.remove(index)
            self.start_next()
        return self.scratch[index]


GROUPS = [(group, part) for group in range(4) for part in range(2)]


def halves(x):
    high = x.astype(BF)
    return high, (x - high.astype(F32)).astype(BF)


def lanes_like(x):
    return lax.broadcasted_iota(jnp.int32, x.shape, x.ndim - 1)


def flip_shift(x):
    lanes = lanes_like(x)
    return jnp.take_along_axis(x, (128 - lanes) % 128, axis=-1)


def block(x, q):
    return x[:, 128 * q : 128 * (q + 1)]


def mirrored(x, top, count, keep_first):
    out = []
    for q in range(count):
        body = flip_shift(block(x, top - 1 - q))
        first = lanes_like(body) == 0
        if q == 0 and not keep_first:
            out.append(jnp.where(first, 0.0, body))
        else:
            out.append(jnp.where(first, block(x, top - q), body))
    return jnp.concatenate(out, axis=1)


NT = (((1,), (1,)), ((), ()))
NN = (((1,), (0,)), ((), ()))
TN = (((0,), (0,)), ((), ()))


def dot(a, b, dims=NN):
    return lax.dot_general(a, b, dims, preferred_element_type=F32)


def fold(grid):
    q = grid.shape[1] // 4
    blocks = q // 128
    rows = grid.shape[0]
    zero = jnp.zeros((rows, 128), F32)
    a = grid[:, : q + 128]
    c = grid[:, 2 * q : 3 * q + 128]
    b = jnp.concatenate([mirrored(grid, 2 * blocks, blocks, False), zero], axis=1)
    d = jnp.concatenate([mirrored(grid, 4 * blocks, blocks, False), zero], axis=1)
    ac, bd, amc, bmd = a + c, b + d, a - c, b - d
    return ac + bd, ac - bd, amc - bmd, amc + bmd


def analyse(grid, table, perm):
    rows = grid.shape[0]
    pad = jnp.zeros((64 - rows, grid.shape[1] // 4 + 128), BF)
    parts = fold(grid)
    natural = []
    for parity in (0, 1):
        sums = []
        for c in (0, 1):
            high, low = halves(parts[2 * parity + c])
            both = jnp.concatenate([high, pad, low, pad], axis=0)
            if c == 1:
                both = jnp.concatenate([low, pad, high, pad], axis=0)
            acc = dot(table[2 * parity + c, 0], both, NT) + dot(table[2 * parity + c, 1], both, NT)
            sums.append(acc + pltpu.roll(acc, 64, 1))
        natural.append(jnp.where(lanes_like(sums[0]) < 64, sums[0], sums[1]))
    natural = jnp.concatenate(natural, axis=0)
    high, low = halves(natural)
    moved = dot(perm, jnp.concatenate([high, low], axis=1))
    return moved[:, :128] + moved[:, 128:]


def place_of(wave, waves):
    return wave // 2 + (wave % 2) * (waves // 2)


def to_natural(order_row):
    waves = order_row.shape[1]
    hit = lax.broadcasted_iota(jnp.int32, (waves, waves), 0) == place_of(order_row, waves)
    return hit.astype(F32).astype(BF)


def to_slots(order_row):
    waves = order_row.shape[1]
    place = jnp.broadcast_to(place_of(order_row, waves).astype(F32), (128, waves)).T
    lanes = lanes_like(place)
    hits = [(place == (lanes + first).astype(F32)).astype(F32).astype(BF) for first in range(0, waves, 128)]
    return jnp.concatenate(hits, axis=1)


def synthesise(band, table, perm_t, rows, lon):
    q = lon // 4
    blocks = q // 128
    waves = band.shape[0]
    high, low = halves(band)
    moved = dot(perm_t, jnp.concatenate([high, low], axis=1))
    natural = moved[:, :128] + moved[:, 128:]
    parts = []
    for parity in (0, 1):
        flipped = natural[parity * (waves // 2) : (parity + 1) * (waves // 2)].T
        high, low = halves(flipped)
        for c in (0, 1):
            lhs = jnp.concatenate([high[64 * c : 64 * c + 64], low[64 * c : 64 * c + 64]], axis=0)
            acc = dot(lhs, table[2 * parity + c, 0]) + dot(lhs, table[2 * parity + c, 1])
            parts.append(acc[:rows] + acc[64 : 64 + rows])
    ce, se, co, so = parts
    f1 = (ce + co + se + so)[:, :q]
    a = ce - co - se + so
    f3 = (ce - co + se - so)[:, :q]
    b = ce + co - se - so
    f2 = mirrored(a, blocks, blocks, True)
    f4 = mirrored(b, blocks, blocks, True)
    return jnp.concatenate([f1, f2, f3, f4], axis=1)


def turn(x, by):
    return pltpu.roll(x, by % 128, 1)


def pack(x):
    lanes = lanes_like(x)
    y = jnp.where(lanes < 48, x, turn(x, -16))
    k = x.shape[0] // 4
    a, b, c, d = (y[i * k : (i + 1) * k] for i in range(4))
    lanes = lanes[:k]
    return jnp.concatenate(
        [
            jnp.where(lanes < 96, a, turn(b, 96)),
            jnp.where(lanes < 64, turn(b, -32), turn(c, 64)),
            jnp.where(lanes < 32, turn(c, -64), turn(d, 32)),
        ],
        axis=0,
    )


def unpack(p):
    k = p.shape[0] // 3
    p0, p1, p2 = (p[i * k : (i + 1) * k] for i in range(3))
    lanes = lanes_like(p0)
    y = jnp.concatenate(
        [
            p0,
            jnp.where(lanes < 32, turn(p0, 32), turn(p1, 32)),
            jnp.where(lanes < 64, turn(p1, 64), turn(p2, 64)),
            turn(p2, -32),
        ],
        axis=0,
    )
    lanes = lanes_like(y)
    x = jnp.where(lanes < 48, y, turn(y, 16))
    return jnp.where((lanes < 48) | ((lanes >= 64) & (lanes < 112)), x, 0.0)


def total(x):
    return jnp.sum(jnp.sum(x, axis=0, keepdims=True), axis=1, keepdims=True)


def mark(x, values):
    rows = lax.broadcasted_iota(jnp.int32, x.shape, x.ndim - 2)
    lanes = lanes_like(x)
    for i, value in enumerate(values):
        value = value.reshape((1,) * x.ndim)
        x = jnp.where((rows == 0) & (lanes == 48 + i), value, x)
    return x


def spread(values, level):
    lanes = lax.broadcasted_iota(jnp.int32, (1, 128), 1)
    out = jnp.zeros((1, 128), F32)
    for i, value in enumerate(values):
        out = jnp.where(lanes == 8 * i + level, value, out)
    return out


def quantities(row, count):
    lanes = lanes_like(row)
    return [jnp.where(lanes < 8, turn(row, -8 * i), 0.0) for i in range(count)]


def level_sum(members_ref, level, held, semaphores):
    count = members_ref.shape[0]
    copies = [pltpu.make_async_copy(members_ref.at[k, level], held.at[k], semaphores.at[k]) for k in range(count)]
    for copy in copies:
        copy.start()

    def finish():
        acc = None
        for k in range(count):
            copies[k].wait()
            value = held[k].astype(F32)
            acc = value if acc is None else acc + value
        return acc

    return finish


PIECES = 3


def other_kernel(grp_ref, members_ref, count_ref, order_ref, table_ref, out_ref, sum_ref, held, held_table, held_count, sums_sem, table_sem, count_sem):
    summed = level_sum(members_ref, 1 - grp_ref[0], held, sums_sem)
    count = pltpu.make_async_copy(count_ref, held_count, count_sem)
    count.start()
    table = Loaded(table_ref, held_table, table_sem, GROUPS)
    perm = to_slots(order_ref[...].reshape(1, order_ref.shape[0]))
    acc = summed()
    sum_ref[...] = acc
    count.wait()
    weights = held_count[...].astype(F32) * 0.5
    out_ref[...] = pack(analyse(-weights * (acc / MEM), table, perm))


def own_kernel(grp_ref, members_ref, obs_ref, count_ref, row_ref, table_ref, sum_other_ref, out_ref, sums_ref, held, held_table, held_obs, sums_sem, table_sem, obs_sem):
    summed = level_sum(members_ref, grp_ref[0], held, sums_sem)
    obs = pltpu.make_async_copy(obs_ref.at[grp_ref[0]], held_obs, obs_sem)
    obs.start()
    table = Loaded(table_ref, held_table, table_sem, GROUPS)
    perm = to_slots(row_ref[...])
    acc = summed()
    sums_ref[0] = sum_other_ref[...]
    sums_ref[1] = acc
    weights = count_ref[...].astype(F32) * 0.5
    obs.wait()
    out_ref[...] = analyse(weights * (held_obs[...] - acc / MEM), table, perm)


def join_kernel(own_ref, packed_ref, out_ref):
    out_ref[...] = (own_ref[...] + unpack(packed_ref[...])).reshape(out_ref.shape)


LAT_GROUPS = [(parity, part) for parity in range(2) for part in range(2)]


def southern(x, rows):
    lanes = lanes_like(x)
    index = jnp.where(lanes < rows, rows - 1 - lanes, jnp.where((lanes >= 64) & (lanes < 64 + rows), 127 + rows - lanes, lanes))
    return jnp.take_along_axis(x, index, axis=-1)


def side_by_side(chunks):
    lower = lanes_like(chunks[0]) < 64
    pairs = [(chunks[k], chunks[k + 1]) for k in range(0, len(chunks), 2)]
    cos = [jnp.where(lower, x0, turn(x1, 64)) for x0, x1 in pairs]
    sin = [jnp.where(lower, turn(x0, 64), x1) for x0, x1 in pairs]
    return jnp.concatenate([jnp.concatenate(cos, axis=1), jnp.concatenate(sin, axis=1)], axis=0)


def apart(y):
    slots = y.shape[0] // 2
    out = []
    for p in range(y.shape[1] // 128):
        y0, y1 = block(y[:slots], p), block(y[slots:], p)
        lower = lanes_like(y0) < 64
        out += [jnp.where(lower, y0, turn(y1, 64)), jnp.where(lower, turn(y0, 64), y1)]
    return out


def latitude_analysis(chunks_ref, lat, rows):
    bands, slots, _ = chunks_ref.shape
    north = [chunks_ref[t] for t in range(bands // 2)]
    south = [southern(chunks_ref[bands - 1 - t], rows) for t in range(bands // 2)]
    out = []
    for parity in range(2):
        x = side_by_side([a + b if parity == 0 else a - b for a, b in zip(north, south)])
        lhs = jnp.concatenate(halves(x), axis=0)
        acc = dot(lhs, lat[parity, 0], NT) + dot(lhs, lat[parity, 1], NT)
        out.append(acc[: 2 * slots] + acc[2 * slots :])
    return jnp.concatenate(out, axis=1)


def latitude_synthesis(vector, lat, out_ref, values, rows):
    bands, slots, _ = out_ref.shape
    half = vector.shape[1] // 2
    y = []
    for parity in range(2):
        lhs = jnp.concatenate(halves(vector[:, parity * half : (parity + 1) * half]), axis=0)
        acc = dot(lhs, lat[parity, 0]) + dot(lhs, lat[parity, 1])
        y.append(acc[: 2 * slots] + acc[2 * slots :])
    for t, chunk in enumerate(apart(y[0] + y[1])):
        out_ref[t] = mark(chunk, values)
    for t, chunk in enumerate(apart(y[0] - y[1])):
        out_ref[bands - 1 - t] = mark(southern(chunk, rows), values)


def scale_of(variance, waves_col, degrees):
    slots = waves_col.shape[0]
    lane = lax.broadcasted_iota(jnp.int32, (slots, degrees), 1)
    degree = 2 * (lane % (degrees // 2)) + lane // (degrees // 2)
    scale = jnp.where(degree >= waves_col, jnp.sqrt(variance), 0.0)
    return jnp.concatenate([scale, scale], axis=0)


def latitude_first_kernel(chunks_ref, variance_ref, waves_ref, lat_ref, *refs):
    rhs_ref, out_ref, held, semaphores = refs[-4:]
    lat = Loaded(lat_ref, held, semaphores, LAT_GROUPS)
    scale = scale_of(variance_ref[...], waves_ref[...], variance_ref.shape[1])
    rhs = latitude_analysis(chunks_ref, lat, ROWS) * scale
    rhs_ref[...] = rhs
    latitude_synthesis(rhs * scale, lat, out_ref, [total(rhs * rhs)], ROWS)


def latitude_second_kernel(chunks_ref, variance_ref, waves_ref, rhs_ref, lat_ref, *refs):
    image_ref, out_ref, quotient_ref, held, semaphores = refs[-5:]
    lat = Loaded(lat_ref, held, semaphores, LAT_GROUPS)
    norm, field_norm = chunks_ref[0, 0:1, 49:50], marks(chunks_ref, 48)
    extra = jnp.where(norm > 0.0, field_norm / norm, 0.0)
    quotient_ref[...] = jnp.broadcast_to(1.0 + extra, (8, 128))
    scale = scale_of(variance_ref[...], waves_ref[...], variance_ref.shape[1])
    image = latitude_analysis(chunks_ref, lat, ROWS) * scale - extra * rhs_ref[...]
    image_ref[...] = image
    latitude_synthesis(image * scale, lat, out_ref, [], ROWS)


def marks(band_ref, lane):
    value = jnp.zeros((1, 1), F32)
    for t in range(band_ref.shape[0]):
        value = value + band_ref[t, 0:1, lane : lane + 1]
    return value


def grid_kernel(band_ref, count_ref, row_ref, table_ref, *refs):
    field_ref, out_ref, held, semaphores = refs[-4:]
    table = Loaded(table_ref, held, semaphores, GROUPS, ahead=len(GROUPS))
    bands, slots, _ = band_ref.shape
    rows, lon = count_ref.shape
    row = row_ref[...]
    field = synthesise(band_ref[...].reshape(bands * slots, 128), table, to_natural(row), rows, lon)
    field_ref[...] = field
    weighted = count_ref[...].astype(F32) * 0.5 * field
    out = analyse(weighted, table, to_slots(row)).reshape(bands, slots, 128)
    out_ref[...] = mark(out, [total(weighted * field), marks(band_ref, 48)])


def last_kernel(level_ref, band_ref, count_ref, row_ref, table_ref, field_ref, rhs_ref, image_ref, quotient_ref, *refs):
    next_ref, sums_ref, held, semaphores = refs[-4:]
    table = Loaded(table_ref, held, semaphores, GROUPS, ahead=len(GROUPS))
    bands, slots, _ = band_ref.shape
    rows, lon = count_ref.shape
    rhs, image, start = rhs_ref[...], image_ref[...], field_ref[...]
    weights = count_ref[...].astype(F32) * 0.5
    field = synthesise(band_ref[...].reshape(bands * slots, 128), table, to_natural(row_ref[...]), rows, lon)
    next_ref[...] = field
    weighted = weights * field
    row = spread(
        [
            total(rhs * rhs),
            total(weights * start * start),
            total(image * image),
            total(image * rhs),
            total(weighted * field),
            total(weighted * start),
            quotient_ref[0:1, 0:1] / bands,
        ],
        level_ref[0],
    )
    sums_ref[...] = jnp.broadcast_to(row[None], sums_ref.shape)


def combine_kernel(level_ref, sums_ref, sums_in_ref, rhs_ref, image_ref, first_ref, second_ref, control_ref, packed_ref, factors_ref):
    bands, slots, _ = first_ref.shape
    sums = sums_ref[...] + sums_in_ref[...]
    norm, field_norm, image_norm, cross, next_norm, field_cross, quotient = quantities(sums, 7)

    def over_levels(x):
        return jnp.sum(x, axis=1, keepdims=True)

    norm_all, field_all = over_levels(norm), over_levels(field_norm)
    step = norm_all / (norm_all + field_all)
    keep = 1.0 - step * quotient
    norm_next = over_levels(keep * keep * norm - 2.0 * step * keep * cross + step * step * image_norm)
    field_next = over_levels(keep * keep * field_norm - 2.0 * step * keep * field_cross + step * step * next_norm)
    mixed = over_levels(keep * (norm + field_norm) - step * (cross + field_cross))
    ratio = norm_next / norm_all
    curve = norm_next + field_next + 2.0 * ratio * mixed + ratio * ratio * (norm_all + field_all)
    step_next = norm_next / curve
    mine = lanes_like(keep) == level_ref[0]
    first = over_levels(jnp.where(mine, step + step_next * (keep + ratio), 0.0))
    second = -step_next * step
    control_ref[...] = first * rhs_ref[...] + second * image_ref[...]
    band = first * first_ref[...].reshape(bands * slots, 128) + second * second_ref[...].reshape(bands * slots, 128)
    packed_ref[...] = pack(band)
    lanes = lanes_like(sums)
    factors_ref[...] = jnp.where(lanes == 0, first, jnp.where(lanes == 1, second, 0.0))


class Recentering:
    def __init__(self, members_ref, level, sums, out_ref, scratch):
        self.near, self.near_sums, self.held, near_sem, sums_sem, self.out_sem = scratch
        self.out_ref, self.level = out_ref, level
        rows = members_ref.shape[2]
        self.cut = rows // PIECES
        self.loads = []
        for piece in range(PIECES):
            source = members_ref.at[:, level, pl.ds(piece * self.cut, self.cut)]
            self.loads.append(pltpu.make_async_copy(source, self.near.at[piece], near_sem.at[piece]))
        self.sum_loads = [
            pltpu.make_async_copy(source.at[index], self.near_sums.at[k], sums_sem.at[k]) for k, (source, index) in enumerate(sums)
        ]
        for copy in self.sum_loads + self.loads:
            copy.start()

    def run(self, increment):
        for copy in self.sum_loads:
            copy.wait()
        copies = []
        for piece in range(PIECES):
            here = slice(piece * self.cut, (piece + 1) * self.cut)
            mean = (self.near_sums[0, here] + self.near_sums[1, here]) / MEM
            offset = (mean + increment(here)) - SPREAD_FACTOR * mean
            self.loads[piece].wait()
            for k in range(self.near.shape[1]):
                self.held[piece, k] = (SPREAD_FACTOR * self.near[piece, k].astype(F32) + offset).astype(BF)
            target = self.out_ref.at[:, self.level, pl.ds(piece * self.cut, self.cut)]
            copies.append(pltpu.make_async_copy(self.held.at[piece], target, self.out_sem.at[piece]))
            copies[-1].start()
        for copy in copies:
            copy.wait()


def finish_own_kernel(grp_ref, members_ref, sums_ref, sums_in_ref, factors_ref, start_ref, next_ref, out_ref, *scratch):
    work = Recentering(members_ref, grp_ref[0], ((sums_ref, 1), (sums_in_ref, 0)), out_ref, scratch)
    first, second = factors_ref[0:1, 0:1], factors_ref[0:1, 1:2]
    work.run(lambda here: first * start_ref[here] + second * next_ref[here])


def finish_other_kernel(grp_ref, members_ref, sums_ref, sums_in_ref, packed_ref, row_ref, table_ref, half_ref, out_ref, held_table, table_sem, *scratch):
    table = Loaded(table_ref, held_table, table_sem, GROUPS, ahead=len(GROUPS))
    work = Recentering(members_ref, 1 - grp_ref[0], ((sums_ref, 0), (sums_in_ref, 1)), out_ref, scratch)
    rows, lon = members_ref.shape[2:]
    field = synthesise(unpack(packed_ref[...]), table, to_natural(row_ref[...]), rows, lon)
    work.run(lambda here: field[here])


def shape(*dims):
    return jax.ShapeDtypeStruct(dims, F32)


def call(kernel, outs, name, hbm=(), hbm_outs=(), scalars=(), aliases=None, scratch=(), limit=LARGE_LIMIT):
    def run(*args):
        def space(i, far, scalars=()):
            return pltpu.SMEM if i in scalars else pltpu.HBM if i in far else pltpu.VMEM

        return pl.pallas_call(
            kernel,
            out_shape=outs,
            in_specs=[pl.BlockSpec(memory_space=space(i, hbm, scalars)) for i in range(len(args))],
            out_specs=[pl.BlockSpec(memory_space=space(o, hbm_outs)) for o in range(len(outs))],
            input_output_aliases=aliases or {},
            scratch_shapes=scratch,
            compiler_params=pltpu.CompilerParams(vmem_limit_bytes=limit * 2**20),
            cost_estimate=pl.CostEstimate(flops=1, bytes_accessed=1, transcendentals=0),
            name=name,
        )(*args)

    return run


def on_device(tables, lat_table, members, obs_value, obs_count, variance, wave_order):
    grp = lax.axis_index("grp")
    bands = lax.axis_size("tile")
    levels = lax.axis_size("lev")
    mem, _, rows, lon = members.shape
    waves = wave_order.shape[0]
    slots = waves // bands
    degrees = variance.shape[1]
    swap = [(0, 1), (1, 0)]
    own_waves = lax.dynamic_slice_in_dim(wave_order, lax.axis_index("tile") * slots, slots, 0)[:, None]
    own_variance = lax.dynamic_index_in_dim(variance, grp, 0, keepdims=False)
    own_variance = own_variance.reshape(degrees // 2, 2).T.reshape(1, degrees)
    row = wave_order[None, :]
    grp_scalar = grp[None].astype(jnp.int32)

    chunk = shape(bands, slots, 128)
    packed = shape(waves * 3 // 4, 128)
    field = shape(rows, lon)
    vector = shape(2 * slots, degrees)
    small = shape(8, 128)
    dma = pltpu.SemaphoreType.DMA
    zonal = [pltpu.VMEM(tables.shape, BF), dma((len(GROUPS),))]
    latitude = [pltpu.VMEM(lat_table.shape, BF), dma((len(LAT_GROUPS),))]
    level = pltpu.VMEM((mem, rows, lon), BF)
    cut = rows // PIECES
    level_scalar = (2 * lax.axis_index("lev") + grp)[None].astype(jnp.int32)

    def trade(array):
        return lax.ppermute(array, "grp", swap)

    with jax.named_scope("start"):
        coeffs_other, sum_other = call(
            other_kernel, [packed, field], "other", (1, 2, 4), scalars=(0,), scratch=[level, zonal[0], pltpu.VMEM((rows, lon), jnp.int32), dma((mem,)), zonal[1], dma]
        )(grp_scalar, members, obs_count, wave_order, tables)
        coeffs_in = trade(coeffs_other)
        coeffs_own, sums = call(
            own_kernel,
            [shape(waves, 128), shape(2, rows, lon)],
            "own",
            (1, 2, 5),
            scalars=(0,),
            scratch=[level, zonal[0], pltpu.VMEM((rows, lon), F32), dma((mem,)), zonal[1], dma],
        )(grp_scalar, members, obs_value, obs_count, row, tables, sum_other)
        (coeffs,) = call(join_kernel, [chunk], "join")(coeffs_own, coeffs_in)
        sums_in = trade(sums)

    def exchange(chunks):
        return lax.all_to_all(chunks, "tile", 0, 0, tiled=True)

    with jax.named_scope("solve"):
        rhs, lat_values = call(latitude_first_kernel, [vector, chunk], "lat1", (3,), scratch=latitude)(
            exchange(coeffs), own_variance, own_waves, lat_table
        )
        band_first = exchange(lat_values)
        field_own, coeffs = call(grid_kernel, [field, chunk], "grid", (3,), scratch=zonal)(
            band_first, obs_count, row, tables
        )
        image, lat_values, quotient = call(latitude_second_kernel, [vector, chunk, small], "lat2", (4, 5), scratch=latitude)(
            exchange(coeffs), own_variance, own_waves, rhs, lat_table, sums_in
        )
        band_second = exchange(lat_values)
        sum_row = jax.ShapeDtypeStruct((bands, 1, 128), F32)
        next_own, scalars = call(last_kernel, [field, sum_row], "last", (4,), scalars=(0,), scratch=zonal)(
            level_scalar, band_second, obs_count, row, tables, field_own, rhs, image, quotient
        )
        scalars = jnp.sum(exchange(scalars), axis=0)
        for step in (1, 2):
            scalars = scalars + lax.ppermute(scalars, "lev", [(i, i ^ step) for i in range(levels)])

    with jax.named_scope("finish"):
        control, control_band, factors = call(combine_kernel, [vector, packed, shape(1, 128)], "combine", scalars=(0,), limit=16)(
            level_scalar, scalars, trade(scalars), rhs, image, band_first, band_second
        )
        control_band = trade(control_band)
        near = pltpu.VMEM((PIECES, mem, cut, lon), BF)
        scratch = [near, pltpu.VMEM((2, rows, lon), F32), near, dma((PIECES,)), dma((2,)), dma((PIECES,))]
        whole_out = jax.ShapeDtypeStruct(members.shape, BF)
        (half,) = call(finish_own_kernel, [whole_out], "finish_own", (1, 2, 3), (0,), scalars=(0,), scratch=scratch)(
            grp_scalar, members, sums, sums_in, factors, field_own, next_own
        )
        (recentered,) = call(
            finish_other_kernel, [whole_out], "finish_other", (1, 2, 3, 6, 7), (0,), scalars=(0,), aliases={7: 0}, scratch=zonal + scratch
        )(grp_scalar, members, sums, sums_in, control_band, row, tables, half)
    control = control.reshape(2 * slots, 2, degrees // 2).swapaxes(1, 2)
    return recentered, control.reshape(1, 1, 2, slots, degrees)


def solution(mesh):
    bands = mesh.shape["tile"]
    waves, degrees, rows, lon = 768, 768, 48, 3072
    tables = zonal_tables(waves, lon)
    lat_table = latitude_table(degrees, bands, rows)
    placed = (
        P("grp", "lev", "tile", None),
        P("lev", "tile", None),
        P("tile", None),
        P("lev", None),
        P(),
    )
    return jax.shard_map(
        lambda *args: on_device(jnp.asarray(tables), jnp.asarray(lat_table), *args),
        mesh=mesh,
        in_specs=placed,
        out_specs=(P("grp", "lev", "tile", None), P("lev", "grp", None, "tile", None)),
        check_vma=False,
    )
```
